32 devices in a mesh: gx: 8 (over z, y), gy: 4 (over x, core).
Axes of the slice: x: 2, y: 2, z: 4, core: 2. Of those that a mesh axis runs over, the one named last changes fastest.
Arguments:
- prediction: float32 [64, 64, 256], P('gx', 'gy'), may hold values from 0 to 1
- vessel_mask: int32 [64, 64, 256], P('gx', 'gy'), may hold values from 0 to 1
Outputs:
- grad_pred: float32 [64, 64, 256], P('gx', 'gy')
- loss: float32 [], replicated
The draws below stay inside these ranges and needn't reach their ends.
All inputs are finite; a program needn't handle non-finite values.
Results may differ from the reference program's by a relative error of at most 0.00002.
Values sent between devices are 32-bit elements; how exact they have to be, the bound alone decides.
No kernel may reach another device: no remote copies, remote signals or barrier semaphores. Data moves between devices by JAX's collectives and lax.ppermute only.
A program may use at most 64 MiB of HBM per device.

```python
import jax
import jax.numpy as jnp
from jax import lax

ITERS = 3
NX = 64
NY = 64
NZ = 256


def vessel_labels(key):
    level = jax.random.randint(key, (NX, NY, NZ), 0, 4 * NX)
    row_ids = lax.broadcasted_iota(jnp.int32, (NX, NY, NZ), 0)
    return (level < NX + 2 * row_ids).astype(jnp.int32)


def draw_vessel_mask(key, part):
    return vessel_labels(key)


def draw_prediction(key, part):
    labels = vessel_labels(key).astype(jnp.float32)
    key = jax.random.fold_in(key, 11)
    noise = 1.5 * jax.random.normal(key, (NX, NY, NZ), jnp.float32)
    return jax.nn.sigmoid(1.5 * (2.0 * labels - 1.0) + noise)


def setup_inputs(seed: int = 0) -> dict:
    splits = jax.random.split(jax.random.key(seed), 3)
    prediction = draw_prediction(jax.random.fold_in(splits[2], 71), 0)
    vessel_mask = draw_vessel_mask(jax.random.fold_in(splits[2], 71), 0)
    return {"prediction": prediction, "vessel_mask": vessel_mask}


softness_factor = 0.1

def window_sum(value_entries):
    padded = jnp.pad(value_entries, ((1, 1), (1, 1), (0, 0)))
    along = padded[:-2] + padded[1:-1] + padded[2:]
    across = along[:, :-2] + along[:, 1:-1] + along[:, 2:]
    blank = jnp.zeros_like(across[..., :1])
    return across + jnp.concatenate([across[..., 1:], blank], -1) + jnp.concatenate([blank, across[..., :-1]], -1)

def erode(value_entries):
    return -softness_factor * jnp.log(window_sum(jnp.exp(-value_entries / softness_factor)))

def dilate(value_entries):
    return softness_factor * jnp.log(window_sum(jnp.exp(value_entries / softness_factor)))

def smooth_rect(value_entries):
    return softness_factor * jax.nn.softplus(value_entries / softness_factor)

def skeleton_of(field):
    image_batch = [field]
    for level_index in range(ITERS + 1):
        image_batch.append(erode(image_batch[-1]))
    skeleton = smooth_rect(image_batch[0] - dilate(image_batch[1]))
    for level_index in range(1, ITERS + 1):
        delta = smooth_rect(image_batch[level_index] - dilate(image_batch[level_index + 1]))
        skeleton = skeleton + smooth_rect(delta - skeleton * delta)
    return skeleton

def reference(prediction, vessel_mask):
    mask_field = vessel_mask.astype(jnp.float32)
    mask_skel = skeleton_of(mask_field)

    def loss_of(predicted):
        pred_skel = skeleton_of(predicted)
        precision = (jnp.sum(pred_skel * mask_field) + 1.0) / (jnp.sum(pred_skel) + 1.0)
        sensitivity = (jnp.sum(mask_skel * predicted) + 1.0) / (jnp.sum(mask_skel) + 1.0)
        return 1.0 - 2.0 * precision * sensitivity / (precision + sensitivity)
    loss_value, pullback = jax.vjp(loss_of, prediction)
    gradient, = pullback(jnp.ones_like(loss_value))
    return (gradient * (NX * NY * NZ), loss_value)
```

```python
import jax
import jax.numpy as jnp
from jax import lax
from jax.sharding import PartitionSpec as P

ITERS = 3
LEVELS = ITERS + 1
REACH = LEVELS + 1
softness_factor = 0.1


def shifted(block, axis, step):
    count = lax.axis_size(axis)
    pairs = [(i, i + step) for i in range(count) if 0 <= i + step < count]
    return lax.ppermute(block, axis, pairs)


def swapped(block, axis):
    count = lax.axis_size(axis)
    return lax.ppermute(block, axis, [(i, i ^ 1) for i in range(count)])


def with_halo(prediction, mask_field):
    rows, cols, _ = prediction.shape
    wide, thin = 2 * REACH, REACH
    odd = lax.rem(lax.axis_index("gx"), 2) == 1
    other = swapped(jnp.concatenate([prediction, mask_field], 0), "gx")
    other_pred, other_mask = other[:rows], other[rows:]
    low_pred = jnp.where(odd, other_pred, prediction)
    high_pred = jnp.where(odd, prediction, other_pred)
    low_mask = jnp.where(odd, other_mask, mask_field)
    high_mask = jnp.where(odd, mask_field, other_mask)
    pair_pred = jnp.concatenate([low_pred, high_pred], 0)
    pair_mask = jnp.concatenate([low_mask, high_mask], 0)
    below = shifted(jnp.concatenate([pair_pred[-wide:], pair_mask[-thin:]], 0), "gx", 2)
    above = shifted(jnp.concatenate([pair_pred[:wide], pair_mask[:thin]], 0), "gx", -2)
    all_pred = jnp.concatenate([below[:wide], pair_pred, above[:wide]], 0)
    all_mask = jnp.concatenate([below[wide:], pair_mask, above[wide:]], 0)
    tall_pred = jnp.where(odd, all_pred[rows : 2 * rows + 2 * wide], all_pred[: rows + 2 * wide])
    tall_mask = jnp.where(odd, all_mask[rows : 2 * rows + 2 * thin], all_mask[: rows + 2 * thin])

    def edge(lo_pred, lo_mask):
        return jnp.concatenate([jnp.swapaxes(lo_pred, 0, 1), jnp.pad(jnp.swapaxes(lo_mask, 0, 1), ((0, 0), (0, 0), (0, 0)))], 0)

    tall = tall_pred.shape[0]
    short = tall_mask.shape[0]

    def packed(p, m):
        return jnp.concatenate([p.reshape(tall * wide, -1), m.reshape(short * thin, -1)], 0)

    left = shifted(packed(tall_pred[:, -wide:], tall_mask[:, -thin:]), "gy", 1)
    right = shifted(packed(tall_pred[:, :wide], tall_mask[:, :thin]), "gy", -1)

    def unpacked(b):
        return b[: tall * wide].reshape(tall, wide, -1), b[tall * wide :].reshape(short, thin, -1)

    left_pred, left_mask = unpacked(left)
    right_pred, right_mask = unpacked(right)
    return (
        jnp.concatenate([left_pred, tall_pred, right_pred], 1),
        jnp.concatenate([left_mask, tall_mask, right_mask], 1),
    )


def box(e):
    e = e[:-2] + e[1:-1] + e[2:]
    e = e[:, :-2] + e[:, 1:-1] + e[:, 2:]
    blank = jnp.zeros_like(e[..., :1])
    return e + jnp.concatenate([e[..., 1:], blank], -1) + jnp.concatenate([blank, e[..., :-1]], -1)


def crop(e, by):
    return e[by:-by, by:-by] if by else e


def levels_of(power_term, inside, keep):
    width = keep + REACH
    powers = [power_term * inside(width)]
    for _ in range(LEVELS):
        width -= 1
        powers.append(box(powers[-1]) * inside(width))
    return powers


def local(prediction, vessel_mask):
    rows, cols, depth = prediction.shape
    t = softness_factor
    mask_field = vessel_mask.astype(jnp.float32)
    row0 = lax.axis_index("gx") * rows
    col0 = lax.axis_index("gy") * cols
    row_count = rows * lax.axis_size("gx")
    col_count = cols * lax.axis_size("gy")

    def inside(width):
        r = lax.broadcasted_iota(jnp.int32, (rows + 2 * width, cols + 2 * width, 1), 0) + (row0 - width)
        c = lax.broadcasted_iota(jnp.int32, (rows + 2 * width, cols + 2 * width, 1), 1) + (col0 - width)
        return ((r >= 0) & (r < row_count) & (c >= 0) & (c < col_count)).astype(jnp.float32)

    pred_ext, mask_ext = with_halo(prediction, mask_field)

    def forward(field, keep):
        powers = levels_of(jnp.exp(-field / t), inside, keep)
        full = keep + REACH
        opened, inverse = [], []
        here = inside(keep)
        for k in range(1, LEVELS + 1):
            held = full - k
            inv = jnp.where(inside(held) > 0, 1.0 / powers[k], 0.0)
            inverse.append(inv)
            opened.append(box(crop(inv, held - keep - 1)))
        skel = None
        deltas, slopes, rects, skels = [], [], [], []
        for j in range(LEVELS):
            product = crop(powers[j], full - j - keep) * opened[j]
            product = jnp.where(here > 0, product, 1.0)
            slopes.append(1.0 / (1.0 + product))
            delta = jnp.log(1.0 + 1.0 / product)
            deltas.append(delta)
            if skel is None:
                skel = delta
            else:
                e = jnp.exp(delta * (1.0 - t * skel))
                rects.append(e / (1.0 + e))
                skel = skel + jnp.log(1.0 + e)
            skels.append(skel)
        return powers, inverse, opened, skels, deltas, slopes, rects

    _, _, _, mask_skels, _, _, _ = forward(mask_ext, 0)
    mask_skel = t * mask_skels[-1]
    powers, inverse, opened, skels, deltas, slopes, rects = forward(pred_ext, REACH)
    here = inside(REACH)
    pred_skel = t * crop(skels[-1], REACH)
    rest = here
    weights = [None] * LEVELS
    for j in range(ITERS, 0, -1):
        inner = rest * rects[j - 1]
        weights[j] = inner * (1.0 - t * skels[j - 1]) * slopes[j]
        rest = rest - inner * (t * deltas[j])
    weights[0] = rest * slopes[0]
    full = 2 * REACH

    def backward(seed):
        grown = None
        for k in range(LEVELS, 0, -1):
            spread = box(crop(seed * weights[k - 1] / jnp.where(here > 0, opened[k - 1], 1.0), REACH - k - 1))
            inv = crop(inverse[k - 1], full - k - k)
            part = -inv * inv * spread
            if k < LEVELS:
                part = part + crop(seed * weights[k], REACH - k) * inv + grown
            part = part * inside(k)
            grown = box(part)
        return crop(powers[0], full) * grown + crop(seed * weights[0], REACH)

    by_label = backward(mask_ext)
    by_one = backward(jnp.ones_like(mask_ext))
    sums = jnp.stack(
        [
            jnp.sum(pred_skel * mask_field),
            jnp.sum(pred_skel),
            jnp.sum(mask_skel * prediction),
            jnp.sum(mask_skel),
        ]
    )
    devices = lax.axis_size("gx") * lax.axis_size("gy")
    sent = jnp.broadcast_to(jnp.pad(sums, (0, 124))[None, None], (devices, 1, 128))
    got = lax.all_to_all(sent, ("gx", "gy"), 0, 0)
    totals = jnp.sum(got, (0, 1))
    intersection_pred, mass_pred, intersection_mask, mass_mask = (totals[i] for i in range(4))
    precision = (intersection_pred + 1.0) / (mass_pred + 1.0)
    sensitivity = (intersection_mask + 1.0) / (mass_mask + 1.0)
    paired = precision + sensitivity
    loss_value = 1.0 - 2.0 * precision * sensitivity / paired
    slope_prec = -2.0 * sensitivity * sensitivity / (paired * paired)
    slope_sens = -2.0 * precision * precision / (paired * paired)
    coef_intersection = slope_prec / (mass_pred + 1.0)
    coef_mass = -slope_prec * (intersection_pred + 1.0) / ((mass_pred + 1.0) * (mass_pred + 1.0))
    coef_cross = slope_sens / (mass_mask + 1.0)
    gradient = coef_intersection * by_label + coef_mass * by_one + coef_cross * mask_skel
    return (gradient * float(row_count * col_count * depth), loss_value)


def solution(mesh):
    placed = (P("gx", "gy", None), P("gx", "gy", None))
    return jax.shard_map(
        local, mesh=mesh, in_specs=placed, out_specs=(P("gx", "gy", None), P()), check_vma=False
    )
```

```python
import jax
import jax.numpy as jnp
from jax import lax
from jax.experimental import pallas as pl
from jax.experimental.pallas import tpu as pltpu
from jax.sharding import PartitionSpec as P

ITERS = 3
LEVELS = ITERS + 1
REACH = LEVELS + 1
softness_factor = 0.1


def shifted(block, axis, step):
    count = lax.axis_size(axis)
    pairs = [(i, i + step) for i in range(count) if 0 <= i + step < count]
    return lax.ppermute(block, axis, pairs)


def swapped(block, axis):
    count = lax.axis_size(axis)
    return lax.ppermute(block, axis, [(i, i ^ 1) for i in range(count)])


def with_halo(prediction, mask_field):
    rows, cols, _ = prediction.shape
    wide, thin = 2 * REACH, REACH
    odd = lax.rem(lax.axis_index("gx"), 2) == 1
    other = swapped(jnp.concatenate([prediction, mask_field], 0), "gx")
    other_pred, other_mask = other[:rows], other[rows:]
    low_pred = jnp.where(odd, other_pred, prediction)
    high_pred = jnp.where(odd, prediction, other_pred)
    low_mask = jnp.where(odd, other_mask, mask_field)
    high_mask = jnp.where(odd, mask_field, other_mask)
    pair_pred = jnp.concatenate([low_pred, high_pred], 0)
    pair_mask = jnp.concatenate([low_mask, high_mask], 0)
    below = shifted(jnp.concatenate([pair_pred[-wide:], pair_mask[-thin:]], 0), "gx", 2)
    above = shifted(jnp.concatenate([pair_pred[:wide], pair_mask[:thin]], 0), "gx", -2)
    all_pred = jnp.concatenate([below[:wide], pair_pred, above[:wide]], 0)
    all_mask = jnp.concatenate([below[wide:], pair_mask, above[wide:]], 0)
    tall_pred = jnp.where(odd, all_pred[rows : 2 * rows + 2 * wide], all_pred[: rows + 2 * wide])
    tall_mask = jnp.where(odd, all_mask[rows : 2 * rows + 2 * thin], all_mask[: rows + 2 * thin])

    tall = tall_pred.shape[0]
    short = tall_mask.shape[0]

    def packed(p, m):
        return jnp.concatenate([p.reshape(tall * wide, -1), m.reshape(short * thin, -1)], 0)

    left = shifted(packed(tall_pred[:, -wide:], tall_mask[:, -thin:]), "gy", 1)
    right = shifted(packed(tall_pred[:, :wide], tall_mask[:, :thin]), "gy", -1)

    def unpacked(b):
        return b[: tall * wide].reshape(tall, wide, -1), b[tall * wide :].reshape(short, thin, -1)

    left_pred, left_mask = unpacked(left)
    right_pred, right_mask = unpacked(right)
    return (
        jnp.concatenate([left_pred, tall_pred, right_pred], 1),
        jnp.concatenate([left_mask, tall_mask, right_mask], 1),
    )


WIDE = 2 * REACH
LANES = 128
SUBLANES = 8
VMEM_BYTES = 40 * 1024 * 1024


def tiles_for(count):
    return -(-count // SUBLANES)


def depth_sum(low, high, first, last):
    low_up, high_up = pltpu.roll(low, 1, 1), pltpu.roll(high, 1, 1)
    low_down, high_down = pltpu.roll(low, LANES - 1, 1), pltpu.roll(high, LANES - 1, 1)
    return (
        low + jnp.where(first, 0.0, low_up) + jnp.where(last, high_down, low_down),
        high + jnp.where(first, low_up, high_up) + jnp.where(last, 0.0, high_down),
    )


def rows_box(ref, base, row_shift, col_shift, count, first, last):
    def across(x, h):
        parts = [ref[x + row_shift, h, pl.ds(base + (col_shift + d), SUBLANES), :] for d in range(3)]
        return parts[0] + parts[1] + parts[2]

    older = [across(0, h) for h in range(2)]
    newer = [across(1, h) for h in range(2)]
    for x in range(count):
        newest = [across(x + 2, h) for h in range(2)]
        low, high = (older[h] + newer[h] + newest[h] for h in range(2))
        older, newer = newer, newest
        yield depth_sum(low, high, first, last)


def over_tiles(count, step):
    def body(i, carry):
        step(pl.multiple_of(i * SUBLANES, SUBLANES))
        return carry

    lax.fori_loop(0, tiles_for(count), body, 0)


def skeleton_kernel(rows, cols, place, own_pred, pred, label, by_label, by_one, mask_skel, sums, *scratch):
    t = softness_factor
    scratch = list(scratch)
    powers = scratch[:5]
    inverses = scratch[5:9]
    opened = scratch[9:13]
    weights = scratch[13:17]
    spreads = scratch[17:25]
    parts = scratch[25:33]
    labels, skels = scratch[33:35]
    label_powers = scratch[35:40]
    label_inverses = scratch[40:44]
    label_opened = scratch[44:48]
    row0, col0, row_count, col_count = (place[i] for i in range(4))
    lane = lax.broadcasted_iota(jnp.int32, (SUBLANES, LANES), 1)
    sublane = lax.broadcasted_iota(jnp.int32, (SUBLANES, LANES), 0)
    first, last = lane == 0, lane == LANES - 1

    def column_index(base, width):
        index = sublane + (base + (col0 - width))
        return jnp.where(index < 0, 1 << 20, index)

    def column_limit(x, width):
        row = row0 + (x - width)
        return jnp.where((row >= 0) & (row < row_count), col_count, 0)

    def raise_field(field, powers, inverses, width):
        def start(base):
            index = column_index(base, width)
            for x in range(rows + 2 * width):
                ok = index < column_limit(x, width)
                for h in range(2):
                    value = field[x, pl.ds(base, SUBLANES), h * LANES : (h + 1) * LANES]
                    powers[0][x, h, pl.ds(base, SUBLANES), :] = jnp.where(ok, jnp.exp(value * (-1.0 / t)), 0.0)

        over_tiles(cols + 2 * width, start)
        for level in range(1, LEVELS + 1):
            here = width - level

            def erode(base, level=level, here=here):
                index = column_index(base, here)
                sums_of = rows_box(powers[level - 1], base, 0, 0, rows + 2 * here, first, last)
                for x, pair in enumerate(sums_of):
                    ok = index < column_limit(x, here)
                    for h in range(2):
                        powers[level][x, h, pl.ds(base, SUBLANES), :] = jnp.where(ok, pair[h], 0.0)
                        inverses[level - 1][x, h, pl.ds(base, SUBLANES), :] = jnp.where(ok, 1.0 / pair[h], 0.0)

            over_tiles(cols + 2 * here, erode)

    def open_field(inverses, opened, width, keep):
        for level in range(1, LEVELS + 1):
            shift = width - level - keep - 1

            def dilate(base, level=level, shift=shift):
                sums_of = rows_box(inverses[level - 1], base, shift, shift, rows + 2 * keep, first, last)
                for x, pair in enumerate(sums_of):
                    for h in range(2):
                        opened[level - 1][x, h, pl.ds(base, SUBLANES), :] = pair[h]

            over_tiles(cols + 2 * keep, dilate)

    def chain(power_of, opened_of):
        skel, saved = None, []
        for j in range(LEVELS):
            wide = opened_of(j)
            product = power_of(j) * wide
            over = 1.0 / (wide * (1.0 + product))
            slope = wide * over
            delta = -jnp.log(product * slope)
            if skel is None:
                skel = delta
                saved.append((slope, over, delta, None, None))
            else:
                left = 1.0 - t * skel
                e = jnp.exp(delta * left)
                grown = 1.0 + e
                saved.append((slope, over, delta, left, e / grown))
                skel = skel + jnp.log(grown)
        return skel, saved

    raise_field(label, label_powers, label_inverses, REACH)
    open_field(label_inverses, label_opened, REACH, 0)

    def label_chain(base):
        for x in range(rows):
            for h in range(2):
                skel, _ = chain(
                    lambda j: label_powers[j][x + REACH - j, h, pl.ds(base + (REACH - j), SUBLANES), :],
                    lambda j: label_opened[j][x, h, pl.ds(base, SUBLANES), :],
                )
                mask_skel[x, pl.ds(base, SUBLANES), h * LANES : (h + 1) * LANES] = t * skel

    over_tiles(cols, label_chain)

    def spread_label(base):
        for x in range(rows + 2 * REACH):
            for h in range(2):
                labels[x, h, pl.ds(base, SUBLANES), :] = label[x, pl.ds(base, SUBLANES), h * LANES : (h + 1) * LANES]

    over_tiles(cols + 2 * REACH, spread_label)

    raise_field(pred, powers, inverses, WIDE)
    open_field(inverses, opened, WIDE, REACH)

    chunk = 3

    def chain_chunk(base, x0):
        index = column_index(base, REACH)
        for dx in range(chunk):
            x = x0 + dx
            ok = index < column_limit(x, REACH)
            for h in range(2):
                skel, saved = chain(
                    lambda j: powers[j][x + REACH - j, h, pl.ds(base + (REACH - j), SUBLANES), :],
                    lambda j: opened[j][x, h, pl.ds(base, SUBLANES), :],
                )
                skels[x, h, pl.ds(base, SUBLANES), :] = t * skel
                seed = labels[x, h, pl.ds(base, SUBLANES), :]
                rest = jnp.where(ok, 1.0, 0.0)
                for j in range(ITERS, -1, -1):
                    slope, over, delta, left, rect = saved[j]
                    if j:
                        inner = rest * rect
                        scaled = inner * left
                        rest = rest - inner * (t * delta)
                    else:
                        scaled = rest
                    weights[j][x, h, pl.ds(base, SUBLANES), :] = jnp.where(ok, scaled * slope, 0.0)
                    spread = jnp.where(ok, scaled * over, 0.0)
                    spreads[j][x, h, pl.ds(base, SUBLANES), :] = spread
                    spreads[LEVELS + j][x, h, pl.ds(base, SUBLANES), :] = seed * spread

    def chain_tile(base):
        def body(i, carry):
            chain_chunk(base, i * chunk)
            return carry

        lax.fori_loop(0, (rows + 2 * REACH) // chunk, body, 0)

    over_tiles(cols + 2 * REACH, chain_tile)

    for level in range(LEVELS, 0, -1):
        for which in range(2):

            def pull(base, level=level, which=which):
                index = column_index(base, level)
                count = rows + 2 * level
                shift = REACH - level - 1
                spread_sums = rows_box(spreads[which * LEVELS + level - 1], base, shift, shift, count, first, last)
                if level < LEVELS:
                    grown_sums = rows_box(parts[which * LEVELS + level], base, 0, 0, count, first, last)
                for x in range(count):
                    ok = index < column_limit(x, level)
                    spread = next(spread_sums)
                    grown = next(grown_sums) if level < LEVELS else None
                    for h in range(2):
                        off = WIDE - 2 * level
                        inv = inverses[level - 1][x + off, h, pl.ds(base + off, SUBLANES), :]
                        part = -(inv * spread[h])
                        if level < LEVELS:
                            at = REACH - level
                            own = weights[level][x + at, h, pl.ds(base + at, SUBLANES), :]
                            if which:
                                own = own * labels[x + at, h, pl.ds(base + at, SUBLANES), :]
                            part = (part + own) * inv + grown[h]
                        else:
                            part = part * inv
                        parts[which * LEVELS + level - 1][x, h, pl.ds(base, SUBLANES), :] = jnp.where(ok, part, 0.0)

            over_tiles(cols + 2 * level, pull)

    def finish(base, totals):
        totals = list(totals)
        pairs = [rows_box(parts[which * LEVELS], base, 0, 0, rows, first, last) for which in range(2)]
        for x in range(rows):
            grown = [next(p) for p in pairs]
            for h in range(2):
                half = slice(h * LANES, (h + 1) * LANES)
                power = powers[0][x + WIDE, h, pl.ds(base + WIDE, SUBLANES), :]
                own = weights[0][x + REACH, h, pl.ds(base + REACH, SUBLANES), :]
                seed = labels[x + REACH, h, pl.ds(base + REACH, SUBLANES), :]
                by_one[x, pl.ds(base, SUBLANES), half] = power * grown[0][h] + own
                by_label[x, pl.ds(base, SUBLANES), half] = power * grown[1][h] + own * seed
                skel = skels[x + REACH, h, pl.ds(base + REACH, SUBLANES), :]
                other = mask_skel[x, pl.ds(base, SUBLANES), half]
                predicted = own_pred[x, pl.ds(base, SUBLANES), half]
                totals[0] += skel * seed
                totals[1] += skel
                totals[2] += other * predicted
                totals[3] += other
        return tuple(totals)

    nothing = jnp.zeros((SUBLANES, LANES), jnp.float32)
    totals = lax.fori_loop(
        0,
        tiles_for(cols),
        lambda i, c: finish(pl.multiple_of(i * SUBLANES, SUBLANES), c),
        (nothing,) * 4,
    )
    packed = jnp.concatenate([jnp.sum(v, 0, keepdims=True) for v in totals] * 2, 0)
    for i in range(sums.shape[0] // SUBLANES):
        sums[i * SUBLANES : (i + 1) * SUBLANES, :] = packed


def combine_kernel(cells, got, by_label, by_one, mask_skel, gradient, loss):
    total = jnp.zeros((SUBLANES, LANES), jnp.float32)
    for i in range(got.shape[0] // SUBLANES):
        total += got[i * SUBLANES : (i + 1) * SUBLANES, :]
    total = total + pltpu.roll(total, 4, 0)
    total = jnp.broadcast_to(jnp.sum(total, 1, keepdims=True), (SUBLANES, LANES))
    intersection_pred, mass_pred, intersection_mask, mass_mask = (total[i : i + 1] + 1.0 for i in range(4))
    precision = intersection_pred / mass_pred
    sensitivity = intersection_mask / mass_mask
    paired = precision + sensitivity
    loss[0] = jnp.max(1.0 - 2.0 * precision * sensitivity / paired)
    slope_prec = -2.0 * sensitivity * sensitivity / (paired * paired)
    slope_sens = -2.0 * precision * precision / (paired * paired)
    coef_intersection = cells * slope_prec / mass_pred
    coef_mass = -coef_intersection * precision
    coef_cross = cells * slope_sens / mass_mask
    a, b, c = (
        jnp.broadcast_to(jnp.concatenate([v, v], 1), (gradient.shape[1], 2 * LANES))
        for v in (coef_intersection, coef_mass, coef_cross)
    )
    for x in range(gradient.shape[0]):
        gradient[x] = a * by_label[x] + b * by_one[x] + c * mask_skel[x]


def local(prediction, vessel_mask):
    rows, cols, depth = prediction.shape
    mask_field = vessel_mask.astype(jnp.float32)
    gx, gy = lax.axis_size("gx"), lax.axis_size("gy")
    place = jnp.stack(
        [lax.axis_index("gx") * rows, lax.axis_index("gy") * cols, jnp.int32(gx * rows), jnp.int32(gy * cols)]
    ).astype(jnp.int32)
    pred_ext, mask_ext = with_halo(prediction, mask_field)

    def held(width, margin=2):
        return pltpu.VMEM((rows + 2 * width, 2, tiles_for(cols + 2 * width + margin + 6) * SUBLANES, LANES), jnp.float32)

    scratch = (
        [held(WIDE - k) for k in range(LEVELS + 1)]
        + [held(WIDE - k) for k in range(1, LEVELS + 1)]
        + [held(REACH)] * 4
        + [held(REACH)] * 4
        + [held(REACH)] * 8
        + [held(k) for k in range(1, LEVELS + 1)] * 2
        + [held(REACH)] * 2
        + [held(REACH - k) for k in range(LEVELS + 1)]
        + [held(REACH - k) for k in range(1, LEVELS + 1)]
        + [held(0)] * 4
    )
    block = jax.ShapeDtypeStruct((rows, cols, depth), jnp.float32)
    vmem = pl.BlockSpec(memory_space=pltpu.VMEM)
    smem = pl.BlockSpec(memory_space=pltpu.SMEM)
    pad = tiles_for(cols + 2 * WIDE) * SUBLANES - (cols + 2 * WIDE)
    pred_ext = jnp.pad(pred_ext, ((0, 0), (0, pad), (0, 0)))
    pad = tiles_for(cols + 2 * REACH) * SUBLANES - (cols + 2 * REACH)
    mask_ext = jnp.pad(mask_ext, ((0, 0), (0, pad), (0, 0)))
    by_label, by_one, mask_skel, sums = pl.pallas_call(
        lambda *refs: skeleton_kernel(rows, cols, *refs),
        out_shape=[block, block, block, jax.ShapeDtypeStruct((gx * gy * 4, LANES), jnp.float32)],
        in_specs=[smem, vmem, vmem, vmem],
        out_specs=[vmem] * 4,
        scratch_shapes=scratch,
        compiler_params=pltpu.CompilerParams(vmem_limit_bytes=VMEM_BYTES),
        name="skeleton",
    )(place, prediction, pred_ext, mask_ext)
    got = lax.all_to_all(sums, ("gx", "gy"), 0, 0, tiled=True)
    gradient, loss = pl.pallas_call(
        lambda *refs: combine_kernel(float(gx * rows * gy * cols * depth), *refs),
        out_shape=[block, jax.ShapeDtypeStruct((1,), jnp.float32)],
        in_specs=[vmem] * 4,
        out_specs=[vmem, smem],
        name="combine",
    )(got, by_label, by_one, mask_skel)
    return (gradient, loss[0])


def solution(mesh):
    placed = (P("gx", "gy", None), P("gx", "gy", None))
    return jax.shard_map(
        local, mesh=mesh, in_specs=placed, out_specs=(P("gx", "gy", None), P()), check_vma=False
    )
```

```python
import jax
import jax.numpy as jnp
from jax import lax
from jax.experimental import pallas as pl
from jax.experimental.pallas import tpu as pltpu
from jax.sharding import PartitionSpec as P

ITERS = 3
LEVELS = ITERS + 1
REACH = LEVELS + 1
softness_factor = 0.1


def moved(block, axis, target):
    count = lax.axis_size(axis)
    pairs = [(i, target(i)) for i in range(count) if 0 <= target(i) < count]
    return lax.ppermute(block, axis, pairs)


def with_halo(packed, rows):
    wide, thin = 2 * REACH, REACH
    rest = wide - rows
    cols = packed.shape[1]
    odd = lax.rem(lax.axis_index("gx"), 2) == 1
    other = moved(packed, "gx", lambda i: i ^ 1)
    own_pred, own_mask = packed[:rows], packed[rows:]
    other_pred, other_mask = other[:rows], other[rows:]
    outer = jnp.where(
        odd,
        jnp.concatenate([other_pred, own_pred[:rest], other_mask[:thin]], 0),
        jnp.concatenate([own_pred[rows - rest :], other_pred, other_mask[rows - thin :]], 0),
    )
    inner = jnp.where(odd, own_pred[rows - rest :], own_pred[:rest])
    far = moved(outer, "gx", lambda i: i - 2 if i % 2 else i + 2)
    near = moved(inner, "gx", lambda i: i + 2 if i % 2 else i - 2)
    tall_pred = jnp.where(
        odd,
        jnp.concatenate([near, other_pred, own_pred, far[:wide]], 0),
        jnp.concatenate([far[:wide], own_pred, other_pred, near], 0),
    )
    tall_mask = jnp.where(
        odd,
        jnp.concatenate([other_mask[rows - thin :], own_mask, far[wide:]], 0),
        jnp.concatenate([far[wide:], own_mask, other_mask[:thin]], 0),
    )
    tall, short = tall_pred.shape[0], tall_mask.shape[0]

    def side(p, m):
        return jnp.concatenate([p.reshape(tall * wide, -1), m.reshape(short * thin, -1)], 0)

    def unside(b):
        return b[: tall * wide].reshape(tall, wide, -1), b[tall * wide :].reshape(short, thin, -1)

    left_pred, left_mask = unside(moved(side(tall_pred[:, -wide:], tall_mask[:, -thin:]), "gy", lambda i: i + 1))
    right_pred, right_mask = unside(moved(side(tall_pred[:, :wide], tall_mask[:, :thin]), "gy", lambda i: i - 1))

    def framed(parts):
        count = sum(p.shape[1] for p in parts)
        return jnp.pad(jnp.concatenate(parts, 1), ((0, 0), (0, tiles_for(count) * SUBLANES - count), (0, 0)))

    return framed([left_pred, tall_pred, right_pred]), framed([left_mask, tall_mask, right_mask])


WIDE = 2 * REACH
LANES = 128
SUBLANES = 8
VMEM_BYTES = 40 * 1024 * 1024


def tiles_for(count):
    return -(-count // SUBLANES)


def depth_sum(low, high, first, last):
    low_up, high_up = pltpu.roll(low, 1, 1), pltpu.roll(high, 1, 1)
    low_down, high_down = pltpu.roll(low, LANES - 1, 1), pltpu.roll(high, LANES - 1, 1)
    return (
        low + jnp.where(first, 0.0, low_up) + jnp.where(last, high_down, low_down),
        high + jnp.where(first, low_up, high_up) + jnp.where(last, 0.0, high_down),
    )


def rows_box(ref, base, row_shift, col_shift, count, first, last):
    def across(x, h):
        parts = [ref[x + row_shift, h, pl.ds(base + (col_shift + d), SUBLANES), :] for d in range(3)]
        return parts[0] + parts[1] + parts[2]

    older = [across(0, h) for h in range(2)]
    newer = [across(1, h) for h in range(2)]
    for x in range(count):
        newest = [across(x + 2, h) for h in range(2)]
        low, high = (older[h] + newer[h] + newest[h] for h in range(2))
        older, newer = newer, newest
        yield depth_sum(low, high, first, last)


def over_tiles(count, step):
    for i in range(tiles_for(count)):
        step(i * SUBLANES)


def skeleton_kernel(rows, cols, place, own_pred, pred, label, results, sums, *scratch):
    t = softness_factor
    scratch = list(scratch)
    by_label, by_one, mask_skel = (results.at[i] for i in range(3))
    powers = scratch[:5]
    inverses = scratch[5:9]
    opened = scratch[9:13]
    weights = scratch[13:17]
    spreads = scratch[17:25]
    parts = scratch[25:33]
    labels, skels = scratch[33:35]
    label_powers = scratch[35:40]
    label_inverses = scratch[40:44]
    label_opened = scratch[44:48]
    row0, col0, row_count, col_count = (place[i] for i in range(4))
    lane = lax.broadcasted_iota(jnp.int32, (SUBLANES, LANES), 1)
    sublane = lax.broadcasted_iota(jnp.int32, (SUBLANES, LANES), 0)
    first, last = lane == 0, lane == LANES - 1

    def column_index(base, width):
        index = sublane + (base + (col0 - width))
        return jnp.where(index < 0, 1 << 20, index)

    def column_limit(x, width):
        row = row0 + (x - width)
        return jnp.where((row >= 0) & (row < row_count), col_count, 0)

    def raise_field(field, powers, inverses, width):
        def start(base):
            index = column_index(base, width)
            for x in range(rows + 2 * width):
                ok = index < column_limit(x, width)
                for h in range(2):
                    value = field[x, pl.ds(base, SUBLANES), h * LANES : (h + 1) * LANES]
                    powers[0][x, h, pl.ds(base, SUBLANES), :] = jnp.where(ok, jnp.exp(value * (-1.0 / t)), 0.0)

        over_tiles(cols + 2 * width, start)
        for level in range(1, LEVELS + 1):
            here = width - level

            def erode(base, level=level, here=here):
                index = column_index(base, here)
                sums_of = rows_box(powers[level - 1], base, 0, 0, rows + 2 * here, first, last)
                for x, pair in enumerate(sums_of):
                    ok = index < column_limit(x, here)
                    for h in range(2):
                        powers[level][x, h, pl.ds(base, SUBLANES), :] = jnp.where(ok, pair[h], 0.0)
                        inverses[level - 1][x, h, pl.ds(base, SUBLANES), :] = jnp.where(ok, 1.0 / pair[h], 0.0)

            over_tiles(cols + 2 * here, erode)

    def open_field(inverses, opened, width, keep):
        for level in range(1, LEVELS + 1):
            shift = width - level - keep - 1

            def dilate(base, level=level, shift=shift):
                sums_of = rows_box(inverses[level - 1], base, shift, shift, rows + 2 * keep, first, last)
                for x, pair in enumerate(sums_of):
                    for h in range(2):
                        opened[level - 1][x, h, pl.ds(base, SUBLANES), :] = pair[h]

            over_tiles(cols + 2 * keep, dilate)

    def chain(power_of, opened_of):
        skel, saved = None, []
        for j in range(LEVELS):
            wide = opened_of(j)
            product = power_of(j) * wide
            over = 1.0 / (wide * (1.0 + product))
            slope = wide * over
            delta = -jnp.log(product * slope)
            if skel is None:
                skel = delta
                saved.append((slope, over, delta, None, None))
            else:
                left = 1.0 - t * skel
                e = jnp.exp(delta * left)
                grown = 1.0 + e
                saved.append((slope, over, delta, left, e / grown))
                skel = skel + jnp.log(grown)
        return skel, saved

    raise_field(label, label_powers, label_inverses, REACH)
    open_field(label_inverses, label_opened, REACH, 0)

    def label_chain(base):
        for x in range(rows):
            for h in range(2):
                skel, _ = chain(
                    lambda j: label_powers[j][x + REACH - j, h, pl.ds(base + (REACH - j), SUBLANES), :],
                    lambda j: label_opened[j][x, h, pl.ds(base, SUBLANES), :],
                )
                mask_skel[x, pl.ds(base, SUBLANES), h * LANES : (h + 1) * LANES] = t * skel

    over_tiles(cols, label_chain)

    def spread_label(base):
        for x in range(rows + 2 * REACH):
            for h in range(2):
                labels[x, h, pl.ds(base, SUBLANES), :] = label[x, pl.ds(base, SUBLANES), h * LANES : (h + 1) * LANES]

    over_tiles(cols + 2 * REACH, spread_label)

    raise_field(pred, powers, inverses, WIDE)
    open_field(inverses, opened, WIDE, REACH)

    chunk = 3

    def chain_chunk(base, x0):
        index = column_index(base, REACH)
        for dx in range(chunk):
            x = x0 + dx
            ok = index < column_limit(x, REACH)
            for h in range(2):
                skel, saved = chain(
                    lambda j: powers[j][x + REACH - j, h, pl.ds(base + (REACH - j), SUBLANES), :],
                    lambda j: opened[j][x, h, pl.ds(base, SUBLANES), :],
                )
                skels[x, h, pl.ds(base, SUBLANES), :] = t * skel
                seed = labels[x, h, pl.ds(base, SUBLANES), :]
                rest = jnp.where(ok, 1.0, 0.0)
                for j in range(ITERS, -1, -1):
                    slope, over, delta, left, rect = saved[j]
                    if j:
                        inner = rest * rect
                        scaled = inner * left
                        rest = rest - inner * (t * delta)
                    else:
                        scaled = rest
                    weights[j][x, h, pl.ds(base, SUBLANES), :] = jnp.where(ok, scaled * slope, 0.0)
                    spread = jnp.where(ok, scaled * over, 0.0)
                    spreads[j][x, h, pl.ds(base, SUBLANES), :] = spread
                    spreads[LEVELS + j][x, h, pl.ds(base, SUBLANES), :] = seed * spread

    def chain_tile(base):
        def body(i, carry):
            chain_chunk(base, i * chunk)
            return carry

        lax.fori_loop(0, (rows + 2 * REACH) // chunk, body, 0)

    over_tiles(cols + 2 * REACH, chain_tile)

    for level in range(LEVELS, 0, -1):
        for which in range(2):

            def pull(base, level=level, which=which):
                index = column_index(base, level)
                count = rows + 2 * level
                shift = REACH - level - 1
                spread_sums = rows_box(spreads[which * LEVELS + level - 1], base, shift, shift, count, first, last)
                if level < LEVELS:
                    grown_sums = rows_box(parts[which * LEVELS + level], base, 0, 0, count, first, last)
                for x in range(count):
                    ok = index < column_limit(x, level)
                    spread = next(spread_sums)
                    grown = next(grown_sums) if level < LEVELS else None
                    for h in range(2):
                        off = WIDE - 2 * level
                        inv = inverses[level - 1][x + off, h, pl.ds(base + off, SUBLANES), :]
                        part = -(inv * spread[h])
                        if level < LEVELS:
                            at = REACH - level
                            own = weights[level][x + at, h, pl.ds(base + at, SUBLANES), :]
                            if which:
                                own = own * labels[x + at, h, pl.ds(base + at, SUBLANES), :]
                            part = (part + own) * inv + grown[h]
                        else:
                            part = part * inv
                        parts[which * LEVELS + level - 1][x, h, pl.ds(base, SUBLANES), :] = jnp.where(ok, part, 0.0)

            over_tiles(cols + 2 * level, pull)

    def finish(base, totals):
        totals = list(totals)
        pairs = [rows_box(parts[which * LEVELS], base, 0, 0, rows, first, last) for which in range(2)]
        for x in range(rows):
            grown = [next(p) for p in pairs]
            for h in range(2):
                half = slice(h * LANES, (h + 1) * LANES)
                power = powers[0][x + WIDE, h, pl.ds(base + WIDE, SUBLANES), :]
                own = weights[0][x + REACH, h, pl.ds(base + REACH, SUBLANES), :]
                seed = labels[x + REACH, h, pl.ds(base + REACH, SUBLANES), :]
                by_one[x, pl.ds(base, SUBLANES), half] = power * grown[0][h] + own
                by_label[x, pl.ds(base, SUBLANES), half] = power * grown[1][h] + own * seed
                skel = skels[x + REACH, h, pl.ds(base + REACH, SUBLANES), :]
                other = mask_skel[x, pl.ds(base, SUBLANES), half]
                predicted = own_pred[x, pl.ds(base, SUBLANES), half]
                totals[0] += skel * seed
                totals[1] += skel
                totals[2] += other * predicted
                totals[3] += other
        return tuple(totals)

    nothing = jnp.zeros((SUBLANES, LANES), jnp.float32)
    totals = (nothing,) * 4
    for i in range(tiles_for(cols)):
        totals = finish(i * SUBLANES, totals)
    packed = jnp.concatenate([jnp.sum(v, 0, keepdims=True) for v in totals] * 2, 0)
    for i in range(sums.shape[0] // SUBLANES):
        sums[i * SUBLANES : (i + 1) * SUBLANES, :] = packed


def combine_kernel(cells, got, results, gradient, loss):
    total = jnp.zeros((SUBLANES, LANES), jnp.float32)
    for i in range(got.shape[0] // SUBLANES):
        total += got[i * SUBLANES : (i + 1) * SUBLANES, :]
    total = total + pltpu.roll(total, 4, 0)
    total = jnp.broadcast_to(jnp.sum(total, 1, keepdims=True), (SUBLANES, LANES))
    intersection_pred, mass_pred, intersection_mask, mass_mask = (total[i : i + 1] + 1.0 for i in range(4))
    precision = intersection_pred / mass_pred
    sensitivity = intersection_mask / mass_mask
    paired = precision + sensitivity
    loss[0] = jnp.max(1.0 - 2.0 * precision * sensitivity / paired)
    slope_prec = -2.0 * sensitivity * sensitivity / (paired * paired)
    slope_sens = -2.0 * precision * precision / (paired * paired)
    coef_intersection = cells * slope_prec / mass_pred
    coef_mass = -coef_intersection * precision
    coef_cross = cells * slope_sens / mass_mask
    a, b, c = (
        jnp.broadcast_to(jnp.concatenate([v, v], 1), (gradient.shape[1], 2 * LANES))
        for v in (coef_intersection, coef_mass, coef_cross)
    )
    for x in range(gradient.shape[0]):
        gradient[x] = a * results[0, x] + b * results[1, x] + c * results[2, x]


def local(prediction, vessel_mask):
    rows, cols, depth = prediction.shape
    packed = jnp.concatenate([prediction, vessel_mask.astype(jnp.float32)], 0)
    gx, gy = lax.axis_size("gx"), lax.axis_size("gy")
    place = jnp.stack(
        [lax.axis_index("gx") * rows, lax.axis_index("gy") * cols, jnp.int32(gx * rows), jnp.int32(gy * cols)]
    ).astype(jnp.int32)
    pred_ext, mask_ext = with_halo(packed, rows)

    def held(width, margin=2):
        return pltpu.VMEM((rows + 2 * width, 2, tiles_for(cols + 2 * width + margin + 6) * SUBLANES, LANES), jnp.float32)

    scratch = (
        [held(WIDE - k) for k in range(LEVELS + 1)]
        + [held(WIDE - k) for k in range(1, LEVELS + 1)]
        + [held(REACH)] * 4
        + [held(REACH)] * 4
        + [held(REACH)] * 8
        + [held(k) for k in range(1, LEVELS + 1)] * 2
        + [held(REACH)] * 2
        + [held(REACH - k) for k in range(LEVELS + 1)]
        + [held(REACH - k) for k in range(1, LEVELS + 1)]
        + [held(0)] * 4
    )
    block = jax.ShapeDtypeStruct((rows, cols, depth), jnp.float32)
    vmem = pl.BlockSpec(memory_space=pltpu.VMEM)
    smem = pl.BlockSpec(memory_space=pltpu.SMEM)
    results, sums = pl.pallas_call(
        lambda *refs: skeleton_kernel(rows, cols, *refs),
        out_shape=[jax.ShapeDtypeStruct((3, rows, cols, depth), jnp.float32), jax.ShapeDtypeStruct((gx * gy * 4, LANES), jnp.float32)],
        in_specs=[smem, vmem, vmem, vmem],
        out_specs=[vmem] * 2,
        scratch_shapes=scratch,
        compiler_params=pltpu.CompilerParams(vmem_limit_bytes=VMEM_BYTES),
        name="skeleton",
    )(place, packed[:rows], pred_ext, mask_ext)
    got = lax.all_to_all(sums, ("gx", "gy"), 0, 0, tiled=True)
    gradient, loss = pl.pallas_call(
        lambda *refs: combine_kernel(float(gx * rows * gy * cols * depth), *refs),
        out_shape=[block, jax.ShapeDtypeStruct((1,), jnp.float32)],
        in_specs=[vmem] * 2,
        out_specs=[vmem, smem],
        name="combine",
    )(got, results)
    return (gradient, loss[0])


def solution(mesh):
    placed = (P("gx", "gy", None), P("gx", "gy", None))
    return jax.shard_map(
        local, mesh=mesh, in_specs=placed, out_specs=(P("gx", "gy", None), P()), check_vma=False
    )
```

```python
import jax
import jax.numpy as jnp
from jax import lax
from jax.experimental import pallas as pl
from jax.experimental.pallas import tpu as pltpu
from jax.sharding import PartitionSpec as P

ITERS = 3
LEVELS = ITERS + 1
REACH = LEVELS + 1
softness_factor = 0.1


def moved(block, axis, target):
    count = lax.axis_size(axis)
    pairs = [(i, target(i)) for i in range(count) if 0 <= target(i) < count]
    return lax.ppermute(block, axis, pairs)


def with_halo(packed, rows):
    wide, thin = 2 * REACH, REACH
    rest = wide - rows
    own_pred, own_mask = packed[:rows], packed[rows:]
    up = moved(jnp.concatenate([own_pred, own_mask[rows - thin :]], 0), "gx", lambda i: i + 1)
    down = moved(jnp.concatenate([own_pred, own_mask[:thin]], 0), "gx", lambda i: i - 1)
    far_up = moved(own_pred[rows - rest :], "gx", lambda i: i + 2)
    far_down = moved(own_pred[:rest], "gx", lambda i: i - 2)
    tall_pred = jnp.concatenate([far_up, up[:rows], own_pred, down[:rows], far_down], 0)
    tall_mask = jnp.concatenate([up[rows:], own_mask, down[rows:]], 0)
    tall, short = tall_pred.shape[0], tall_mask.shape[0]

    def side(p, m):
        return jnp.concatenate([p.reshape(tall * wide, -1), m.reshape(short * thin, -1)], 0)

    def unside(b):
        return b[: tall * wide].reshape(tall, wide, -1), b[tall * wide :].reshape(short, thin, -1)

    left_pred, left_mask = unside(moved(side(tall_pred[:, -wide:], tall_mask[:, -thin:]), "gy", lambda i: i + 1))
    right_pred, right_mask = unside(moved(side(tall_pred[:, :wide], tall_mask[:, :thin]), "gy", lambda i: i - 1))

    def framed(parts):
        count = sum(p.shape[1] for p in parts)
        return jnp.pad(jnp.concatenate(parts, 1), ((0, 0), (0, tiles_for(count) * SUBLANES - count), (0, 0)))

    return framed([left_pred, tall_pred, right_pred]), framed([left_mask, tall_mask, right_mask])


WIDE = 2 * REACH
LANES = 128
SUBLANES = 8
VMEM_BYTES = 40 * 1024 * 1024


def tiles_for(count):
    return -(-count // SUBLANES)


def depth_sum(low, high, first, last):
    low_up, high_up = pltpu.roll(low, 1, 1), pltpu.roll(high, 1, 1)
    low_down, high_down = pltpu.roll(low, LANES - 1, 1), pltpu.roll(high, LANES - 1, 1)
    return (
        low + jnp.where(first, 0.0, low_up) + jnp.where(last, high_down, low_down),
        high + jnp.where(first, low_up, high_up) + jnp.where(last, 0.0, high_down),
    )


def rows_box(ref, base, row_shift, col_shift, count, first, last):
    def across(x, h):
        parts = [ref[x + row_shift, h, pl.ds(base + (col_shift + d), SUBLANES), :] for d in range(3)]
        return parts[0] + parts[1] + parts[2]

    older = [across(0, h) for h in range(2)]
    newer = [across(1, h) for h in range(2)]
    for x in range(count):
        newest = [across(x + 2, h) for h in range(2)]
        low, high = (older[h] + newer[h] + newest[h] for h in range(2))
        older, newer = newer, newest
        yield depth_sum(low, high, first, last)


def over_tiles(count, step):
    for i in range(tiles_for(count)):
        step(i * SUBLANES)


def skeleton_kernel(rows, cols, place, own_pred, pred, label, results, sums, *scratch):
    t = softness_factor
    scratch = list(scratch)
    stage, copied = scratch[48:]
    by_label, by_one, mask_skel = (stage.at[i] for i in range(3))
    copies = [pltpu.make_async_copy(stage.at[i], results.at[i], copied.at[i]) for i in range(3)]
    powers = scratch[:5]
    inverses = scratch[5:9]
    opened = scratch[9:13]
    weights = scratch[13:17]
    spreads = scratch[17:25]
    parts = scratch[25:33]
    labels, skels = scratch[33:35]
    label_powers = scratch[35:40]
    label_inverses = scratch[40:44]
    label_opened = scratch[44:48]
    row0, col0, row_count, col_count = (place[i] for i in range(4))
    lane = lax.broadcasted_iota(jnp.int32, (SUBLANES, LANES), 1)
    sublane = lax.broadcasted_iota(jnp.int32, (SUBLANES, LANES), 0)
    first, last = lane == 0, lane == LANES - 1

    def column_index(base, width):
        index = sublane + (base + (col0 - width))
        return jnp.where(index < 0, 1 << 20, index)

    def column_limit(x, width):
        row = row0 + (x - width)
        return jnp.where((row >= 0) & (row < row_count), col_count, 0)

    def raise_field(field, powers, inverses, width):
        def start(base):
            index = column_index(base, width)
            for x in range(rows + 2 * width):
                ok = index < column_limit(x, width)
                for h in range(2):
                    value = field[x, pl.ds(base, SUBLANES), h * LANES : (h + 1) * LANES]
                    powers[0][x, h, pl.ds(base, SUBLANES), :] = jnp.where(ok, jnp.exp(value * (-1.0 / t)), 0.0)

        over_tiles(cols + 2 * width, start)
        for level in range(1, LEVELS + 1):
            here = width - level

            def erode(base, level=level, here=here):
                index = column_index(base, here)
                sums_of = rows_box(powers[level - 1], base, 0, 0, rows + 2 * here, first, last)
                for x, pair in enumerate(sums_of):
                    ok = index < column_limit(x, here)
                    for h in range(2):
                        powers[level][x, h, pl.ds(base, SUBLANES), :] = jnp.where(ok, pair[h], 0.0)
                        inverses[level - 1][x, h, pl.ds(base, SUBLANES), :] = jnp.where(ok, 1.0 / pair[h], 0.0)

            over_tiles(cols + 2 * here, erode)

    def open_field(inverses, opened, width, keep):
        for level in range(1, LEVELS + 1):
            shift = width - level - keep - 1

            def dilate(base, level=level, shift=shift):
                sums_of = rows_box(inverses[level - 1], base, shift, shift, rows + 2 * keep, first, last)
                for x, pair in enumerate(sums_of):
                    for h in range(2):
                        opened[level - 1][x, h, pl.ds(base, SUBLANES), :] = pair[h]

            over_tiles(cols + 2 * keep, dilate)

    def chain(power_of, opened_of):
        skel, saved = None, []
        for j in range(LEVELS):
            wide = opened_of(j)
            product = power_of(j) * wide
            over = 1.0 / (wide * (1.0 + product))
            slope = wide * over
            delta = -jnp.log(product * slope)
            if skel is None:
                skel = delta
                saved.append((slope, over, delta, None, None))
            else:
                left = 1.0 - t * skel
                e = jnp.exp(delta * left)
                grown = 1.0 + e
                saved.append((slope, over, delta, left, e / grown))
                skel = skel + jnp.log(grown)
        return skel, saved

    raise_field(label, label_powers, label_inverses, REACH)
    open_field(label_inverses, label_opened, REACH, 0)

    def label_chain(base):
        for x in range(rows):
            for h in range(2):
                skel, _ = chain(
                    lambda j: label_powers[j][x + REACH - j, h, pl.ds(base + (REACH - j), SUBLANES), :],
                    lambda j: label_opened[j][x, h, pl.ds(base, SUBLANES), :],
                )
                mask_skel[x, pl.ds(base, SUBLANES), h * LANES : (h + 1) * LANES] = t * skel

    over_tiles(cols, label_chain)
    copies[2].start()

    def spread_label(base):
        for x in range(rows + 2 * REACH):
            for h in range(2):
                labels[x, h, pl.ds(base, SUBLANES), :] = label[x, pl.ds(base, SUBLANES), h * LANES : (h + 1) * LANES]

    over_tiles(cols + 2 * REACH, spread_label)

    raise_field(pred, powers, inverses, WIDE)
    open_field(inverses, opened, WIDE, REACH)

    chunk = 3

    def chain_chunk(base, x0):
        index = column_index(base, REACH)
        for dx in range(chunk):
            x = x0 + dx
            ok = index < column_limit(x, REACH)
            for h in range(2):
                skel, saved = chain(
                    lambda j: powers[j][x + REACH - j, h, pl.ds(base + (REACH - j), SUBLANES), :],
                    lambda j: opened[j][x, h, pl.ds(base, SUBLANES), :],
                )
                skels[x, h, pl.ds(base, SUBLANES), :] = t * skel
                seed = labels[x, h, pl.ds(base, SUBLANES), :]
                rest = jnp.where(ok, 1.0, 0.0)
                for j in range(ITERS, -1, -1):
                    slope, over, delta, left, rect = saved[j]
                    if j:
                        inner = rest * rect
                        scaled = inner * left
                        rest = rest - inner * (t * delta)
                    else:
                        scaled = rest
                    weights[j][x, h, pl.ds(base, SUBLANES), :] = jnp.where(ok, scaled * slope, 0.0)
                    spread = jnp.where(ok, scaled * over, 0.0)
                    spreads[j][x, h, pl.ds(base, SUBLANES), :] = spread
                    spreads[LEVELS + j][x, h, pl.ds(base, SUBLANES), :] = seed * spread

    def chain_tile(base):
        for i in range((rows + 2 * REACH) // chunk):
            chain_chunk(base, i * chunk)

    over_tiles(cols + 2 * REACH, chain_tile)

    for level in range(LEVELS, 0, -1):
        for which in range(2):

            def pull(base, level=level, which=which):
                index = column_index(base, level)
                count = rows + 2 * level
                shift = REACH - level - 1
                spread_sums = rows_box(spreads[which * LEVELS + level - 1], base, shift, shift, count, first, last)
                if level < LEVELS:
                    grown_sums = rows_box(parts[which * LEVELS + level], base, 0, 0, count, first, last)
                for x in range(count):
                    ok = index < column_limit(x, level)
                    spread = next(spread_sums)
                    grown = next(grown_sums) if level < LEVELS else None
                    for h in range(2):
                        off = WIDE - 2 * level
                        inv = inverses[level - 1][x + off, h, pl.ds(base + off, SUBLANES), :]
                        part = -(inv * spread[h])
                        if level < LEVELS:
                            at = REACH - level
                            own = weights[level][x + at, h, pl.ds(base + at, SUBLANES), :]
                            if which:
                                own = own * labels[x + at, h, pl.ds(base + at, SUBLANES), :]
                            part = (part + own) * inv + grown[h]
                        else:
                            part = part * inv
                        parts[which * LEVELS + level - 1][x, h, pl.ds(base, SUBLANES), :] = jnp.where(ok, part, 0.0)

            over_tiles(cols + 2 * level, pull)

    def finish(base, totals):
        totals = list(totals)
        pairs = [rows_box(parts[which * LEVELS], base, 0, 0, rows, first, last) for which in range(2)]
        for x in range(rows):
            grown = [next(p) for p in pairs]
            for h in range(2):
                half = slice(h * LANES, (h + 1) * LANES)
                power = powers[0][x + WIDE, h, pl.ds(base + WIDE, SUBLANES), :]
                own = weights[0][x + REACH, h, pl.ds(base + REACH, SUBLANES), :]
                seed = labels[x + REACH, h, pl.ds(base + REACH, SUBLANES), :]
                by_one[x, pl.ds(base, SUBLANES), half] = power * grown[0][h] + own
                by_label[x, pl.ds(base, SUBLANES), half] = power * grown[1][h] + own * seed
                skel = skels[x + REACH, h, pl.ds(base + REACH, SUBLANES), :]
                other = mask_skel[x, pl.ds(base, SUBLANES), half]
                predicted = own_pred[x, pl.ds(base, SUBLANES), half]
                totals[0] += skel * seed
                totals[1] += skel
                totals[2] += other * predicted
                totals[3] += other
        return tuple(totals)

    nothing = jnp.zeros((SUBLANES, LANES), jnp.float32)
    totals = (nothing,) * 4
    for i in range(tiles_for(cols)):
        totals = finish(i * SUBLANES, totals)
    copies[0].start()
    copies[1].start()
    packed = jnp.concatenate([jnp.sum(v, 0, keepdims=True) for v in totals] * 2, 0)
    for i in range(sums.shape[0] // SUBLANES):
        sums[i * SUBLANES : (i + 1) * SUBLANES, :] = packed
    for copy in copies:
        copy.wait()


def combine_kernel(cells, got, results, gradient, loss):
    total = jnp.zeros((SUBLANES, LANES), jnp.float32)
    for i in range(got.shape[0] // SUBLANES):
        total += got[i * SUBLANES : (i + 1) * SUBLANES, :]
    total = total + pltpu.roll(total, 4, 0)
    total = jnp.broadcast_to(jnp.sum(total, 1, keepdims=True), (SUBLANES, LANES))
    intersection_pred, mass_pred, intersection_mask, mass_mask = (total[i : i + 1] + 1.0 for i in range(4))
    precision = intersection_pred / mass_pred
    sensitivity = intersection_mask / mass_mask
    paired = precision + sensitivity
    loss[0] = jnp.max(1.0 - 2.0 * precision * sensitivity / paired)
    slope_prec = -2.0 * sensitivity * sensitivity / (paired * paired)
    slope_sens = -2.0 * precision * precision / (paired * paired)
    coef_intersection = cells * slope_prec / mass_pred
    coef_mass = -coef_intersection * precision
    coef_cross = cells * slope_sens / mass_mask
    a, b, c = (
        jnp.broadcast_to(jnp.concatenate([v, v], 1), (gradient.shape[1], 2 * LANES))
        for v in (coef_intersection, coef_mass, coef_cross)
    )
    for x in range(gradient.shape[0]):
        gradient[x] = a * results[0, x] + b * results[1, x] + c * results[2, x]


def local(prediction, vessel_mask):
    rows, cols, depth = prediction.shape
    none = (0, 0)
    packed = lax.optimization_barrier(
        jnp.pad(prediction, ((0, rows), none, none)) + jnp.pad(vessel_mask, ((rows, 0), none, none)).astype(jnp.float32)
    )
    gx, gy = lax.axis_size("gx"), lax.axis_size("gy")
    place = jnp.stack(
        [lax.axis_index("gx") * rows, lax.axis_index("gy") * cols, jnp.int32(gx * rows), jnp.int32(gy * cols)]
    ).astype(jnp.int32)
    pred_ext, mask_ext = with_halo(packed, rows)

    def held(width, margin=2):
        return pltpu.VMEM((rows + 2 * width, 2, tiles_for(cols + 2 * width + margin + 6) * SUBLANES, LANES), jnp.float32)

    scratch = (
        [held(WIDE - k) for k in range(LEVELS + 1)]
        + [held(WIDE - k) for k in range(1, LEVELS + 1)]
        + [held(REACH)] * 4
        + [held(REACH)] * 4
        + [held(REACH)] * 8
        + [held(k) for k in range(1, LEVELS + 1)] * 2
        + [held(REACH)] * 2
        + [held(REACH - k) for k in range(LEVELS + 1)]
        + [held(REACH - k) for k in range(1, LEVELS + 1)]
        + [held(0)] * 4
        + [pltpu.VMEM((3, rows, cols, depth), jnp.float32), pltpu.SemaphoreType.DMA((3,))]
    )
    block = jax.ShapeDtypeStruct((rows, cols, depth), jnp.float32)
    vmem = pl.BlockSpec(memory_space=pltpu.VMEM)
    smem = pl.BlockSpec(memory_space=pltpu.SMEM)
    results, sums = pl.pallas_call(
        lambda *refs: skeleton_kernel(rows, cols, *refs),
        out_shape=[jax.ShapeDtypeStruct((3, rows, cols, depth), jnp.float32), jax.ShapeDtypeStruct((gx * gy * 4, LANES), jnp.float32)],
        in_specs=[smem, vmem, vmem, vmem],
        out_specs=[pl.BlockSpec(memory_space=pltpu.HBM), vmem],
        scratch_shapes=scratch,
        compiler_params=pltpu.CompilerParams(vmem_limit_bytes=VMEM_BYTES),
        name="skeleton",
    )(place, packed[:rows], pred_ext, mask_ext)
    got = lax.all_to_all(sums, ("gx", "gy"), 0, 0, tiled=True)
    gradient, loss = pl.pallas_call(
        lambda *refs: combine_kernel(float(gx * rows * gy * cols * depth), *refs),
        out_shape=[block, jax.ShapeDtypeStruct((1,), jnp.float32)],
        in_specs=[vmem] * 2,
        out_specs=[vmem, smem],
        name="combine",
    )(got, results)
    return (gradient, loss[0])


def solution(mesh):
    placed = (P("gx", "gy", None), P("gx", "gy", None))
    return jax.shard_map(
        local, mesh=mesh, in_specs=placed, out_specs=(P("gx", "gy", None), P()), check_vma=False
    )
```

```python
import jax
import jax.numpy as jnp
from jax import lax
from jax.experimental import pallas as pl
from jax.experimental.pallas import tpu as pltpu
from jax.sharding import PartitionSpec as P

ITERS = 3
LEVELS = ITERS + 1
REACH = LEVELS + 1
softness_factor = 0.1


def moved(block, axis, target):
    count = lax.axis_size(axis)
    pairs = [(i, target(i)) for i in range(count) if 0 <= target(i) < count]
    return lax.ppermute(block, axis, pairs)


def with_halo(packed, rows):
    wide, thin = 2 * REACH, REACH
    rest = wide - rows
    own_pred, own_mask = packed[:rows], packed[rows:]
    spot = lax.axis_index("gx")
    odd, upper = lax.rem(spot, 2) == 1, lax.rem(spot, 4) >= 2
    to_up = jnp.concatenate([own_pred, own_mask[rows - thin :]], 0)
    to_down = jnp.concatenate([own_pred, own_mask[:thin]], 0)
    to_far_up, to_far_down = own_pred[rows - rest :], own_pred[:rest]
    a, b, c, d = lax.optimization_barrier(
        (
            jnp.where(odd, to_down, to_up),
            jnp.where(odd, to_up, to_down),
            jnp.where(upper, to_far_down, to_far_up),
            jnp.where(upper, to_far_up, to_far_down),
        )
    )
    a = moved(a, "gx", lambda i: i ^ 1)
    b = moved(b, "gx", lambda i: i + 1 if i % 2 else i - 1)
    c = moved(c, "gx", lambda i: i ^ 2)
    d = moved(d, "gx", lambda i: i + 2 if i % 4 >= 2 else i - 2)
    a, b, c, d = lax.optimization_barrier((a, b, c, d))
    up, down = jnp.where(odd, a, b), jnp.where(odd, b, a)
    far_up, far_down = jnp.where(upper, c, d), jnp.where(upper, d, c)
    tall_pred = jnp.concatenate([far_up, up[:rows], own_pred, down[:rows], far_down], 0)
    tall_mask = jnp.concatenate([up[rows:], own_mask, down[rows:]], 0)
    tall, short = tall_pred.shape[0], tall_mask.shape[0]

    def side(p, m):
        return jnp.concatenate([p.reshape(tall * wide, -1), m.reshape(short * thin, -1)], 0)

    def unside(b):
        return b[: tall * wide].reshape(tall, wide, -1), b[tall * wide :].reshape(short, thin, -1)

    col_odd = lax.rem(lax.axis_index("gy"), 2) == 1
    high = side(tall_pred[:, -wide:], tall_mask[:, -thin:])
    low = side(tall_pred[:, :wide], tall_mask[:, :thin])
    first = moved(jnp.where(col_odd, low, high), "gy", lambda i: i ^ 1)
    second = moved(jnp.where(col_odd, high, low), "gy", lambda i: i + 1 if i % 2 else i - 1)
    first, second = lax.optimization_barrier((first, second))
    left_pred, left_mask = unside(jnp.where(col_odd, first, second))
    right_pred, right_mask = unside(jnp.where(col_odd, second, first))

    def framed(parts):
        count = sum(p.shape[1] for p in parts)
        return jnp.pad(jnp.concatenate(parts, 1), ((0, 0), (0, tiles_for(count) * SUBLANES - count), (0, 0)))

    return framed([left_pred, tall_pred, right_pred]), framed([left_mask, tall_mask, right_mask])


WIDE = 2 * REACH
LANES = 128
SUBLANES = 8
VMEM_BYTES = 40 * 1024 * 1024


def tiles_for(count):
    return -(-count // SUBLANES)


def depth_sum(low, high, first, last):
    low_up, high_up = pltpu.roll(low, 1, 1), pltpu.roll(high, 1, 1)
    low_down, high_down = pltpu.roll(low, LANES - 1, 1), pltpu.roll(high, LANES - 1, 1)
    return (
        low + jnp.where(first, 0.0, low_up) + jnp.where(last, high_down, low_down),
        high + jnp.where(first, low_up, high_up) + jnp.where(last, 0.0, high_down),
    )


def rows_box(ref, base, row_shift, col_shift, count, first, last):
    def across(x, h):
        parts = [ref[x + row_shift, h, pl.ds(base + (col_shift + d), SUBLANES), :] for d in range(3)]
        return parts[0] + parts[1] + parts[2]

    older = [across(0, h) for h in range(2)]
    newer = [across(1, h) for h in range(2)]
    for x in range(count):
        newest = [across(x + 2, h) for h in range(2)]
        low, high = (older[h] + newer[h] + newest[h] for h in range(2))
        older, newer = newer, newest
        yield depth_sum(low, high, first, last)


def over_tiles(count, step):
    def body(i, carry):
        step(i * SUBLANES)
        return carry

    lax.fori_loop(0, tiles_for(count), body, 0, unroll=True)


def skeleton_kernel(rows, cols, place, own_pred, pred, label, results, sums, *scratch):
    t = softness_factor
    scratch = list(scratch)
    stage, sent, copied = scratch[48:]
    mask_skel = stage.at[2]
    copies = [pltpu.make_async_copy(stage.at[i], results.at[i], copied.at[i]) for i in range(3)]
    copies.append(pltpu.make_async_copy(sent, sums, copied.at[3]))
    powers = scratch[:5]
    inverses = scratch[5:9]
    opened = scratch[9:13]
    weights = scratch[13:17]
    spreads = scratch[17:25]
    parts = scratch[25:33]
    labels, skels = scratch[33:35]
    label_powers = scratch[35:40]
    label_inverses = scratch[40:44]
    label_opened = scratch[44:48]
    row0, col0, row_count, col_count = (place[i] for i in range(4))
    lane = lax.broadcasted_iota(jnp.int32, (SUBLANES, LANES), 1)
    sublane = lax.broadcasted_iota(jnp.int32, (SUBLANES, LANES), 0)
    first, last = lane == 0, lane == LANES - 1

    def column_index(base, width):
        index = sublane + (base + (col0 - width))
        return jnp.where(index < 0, 1 << 20, index)

    def column_limit(x, width):
        row = row0 + (x - width)
        return jnp.where((row >= 0) & (row < row_count), col_count, 0)

    def raise_field(field, powers, inverses, width):
        def start(base):
            index = column_index(base, width)
            for x in range(rows + 2 * width):
                ok = index < column_limit(x, width)
                for h in range(2):
                    value = field[x, pl.ds(base, SUBLANES), h * LANES : (h + 1) * LANES]
                    powers[0][x, h, pl.ds(base, SUBLANES), :] = jnp.where(ok, jnp.exp(value * (-1.0 / t)), 0.0)

        over_tiles(cols + 2 * width, start)
        for level in range(1, LEVELS + 1):
            here = width - level

            def erode(base, level=level, here=here):
                index = column_index(base, here)
                sums_of = rows_box(powers[level - 1], base, 0, 0, rows + 2 * here, first, last)
                for x, pair in enumerate(sums_of):
                    ok = index < column_limit(x, here)
                    for h in range(2):
                        powers[level][x, h, pl.ds(base, SUBLANES), :] = jnp.where(ok, pair[h], 0.0)
                        inverses[level - 1][x, h, pl.ds(base, SUBLANES), :] = jnp.where(ok, 1.0 / pair[h], 0.0)

            over_tiles(cols + 2 * here, erode)

    def open_field(inverses, opened, width, keep):
        for level in range(1, LEVELS + 1):
            shift = width - level - keep - 1

            def dilate(base, level=level, shift=shift):
                sums_of = rows_box(inverses[level - 1], base, shift, shift, rows + 2 * keep, first, last)
                for x, pair in enumerate(sums_of):
                    for h in range(2):
                        opened[level - 1][x, h, pl.ds(base, SUBLANES), :] = pair[h]

            over_tiles(cols + 2 * keep, dilate)

    def chain(power_of, opened_of):
        skel, saved = None, []
        for j in range(LEVELS):
            wide = opened_of(j)
            product = power_of(j) * wide
            over = 1.0 / (wide * (1.0 + product))
            slope = wide * over
            delta = -jnp.log(product * slope)
            if skel is None:
                skel = delta
                saved.append((slope, over, delta, None, None))
            else:
                left = 1.0 - t * skel
                e = jnp.exp(delta * left)
                grown = 1.0 + e
                saved.append((slope, over, delta, left, e / grown))
                skel = skel + jnp.log(grown)
        return skel, saved

    raise_field(label, label_powers, label_inverses, REACH)
    open_field(label_inverses, label_opened, REACH, 0)

    def label_chain(base):
        for x in range(rows):
            for h in range(2):
                skel, _ = chain(
                    lambda j: label_powers[j][x + REACH - j, h, pl.ds(base + (REACH - j), SUBLANES), :],
                    lambda j: label_opened[j][x, h, pl.ds(base, SUBLANES), :],
                )
                mask_skel[x, pl.ds(base, SUBLANES), h * LANES : (h + 1) * LANES] = t * skel

    over_tiles(cols, label_chain)
    copies[2].start()

    def spread_label(base):
        for x in range(rows + 2 * REACH):
            for h in range(2):
                labels[x, h, pl.ds(base, SUBLANES), :] = label[x, pl.ds(base, SUBLANES), h * LANES : (h + 1) * LANES]

    over_tiles(cols + 2 * REACH, spread_label)

    raise_field(pred, powers, inverses, WIDE)
    open_field(inverses, opened, WIDE, REACH)

    chunk = 3

    def chain_chunk(base, x0):
        index = column_index(base, REACH)
        for dx in range(chunk):
            x = x0 + dx
            ok = index < column_limit(x, REACH)
            for h in range(2):
                skel, saved = chain(
                    lambda j: powers[j][x + REACH - j, h, pl.ds(base + (REACH - j), SUBLANES), :],
                    lambda j: opened[j][x, h, pl.ds(base, SUBLANES), :],
                )
                skels[x, h, pl.ds(base, SUBLANES), :] = t * skel
                seed = labels[x, h, pl.ds(base, SUBLANES), :]
                rest = jnp.where(ok, 1.0, 0.0)
                for j in range(ITERS, -1, -1):
                    slope, over, delta, left, rect = saved[j]
                    if j:
                        inner = rest * rect
                        scaled = inner * left
                        rest = rest - inner * (t * delta)
                    else:
                        scaled = rest
                    weights[j][x, h, pl.ds(base, SUBLANES), :] = jnp.where(ok, scaled * slope, 0.0)
                    spread = jnp.where(ok, scaled * over, 0.0)
                    spreads[j][x, h, pl.ds(base, SUBLANES), :] = spread
                    spreads[LEVELS + j][x, h, pl.ds(base, SUBLANES), :] = seed * spread

    def chain_tile(base):
        def body(i, carry):
            chain_chunk(base, i * chunk)
            return carry

        lax.fori_loop(0, (rows + 2 * REACH) // chunk, body, 0, unroll=True)

    over_tiles(cols + 2 * REACH, chain_tile)

    totals = [jnp.zeros((SUBLANES, LANES), jnp.float32) for _ in range(4)]
    for base in range(0, cols, SUBLANES):
        for x in range(rows):
            for h in range(2):
                half = slice(h * LANES, (h + 1) * LANES)
                skel = skels[x + REACH, h, pl.ds(base + REACH, SUBLANES), :]
                other = mask_skel[x, pl.ds(base, SUBLANES), half]
                totals[0] += skel * labels[x + REACH, h, pl.ds(base + REACH, SUBLANES), :]
                totals[1] += skel
                totals[2] += other * own_pred[x, pl.ds(base, SUBLANES), half]
                totals[3] += other
    packed = jnp.concatenate([jnp.sum(v, 0, keepdims=True) for v in totals] * 2, 0)
    for i in range(sums.shape[0] // SUBLANES):
        sent[i * SUBLANES : (i + 1) * SUBLANES, :] = packed
    copies[3].start()

    for which in range(2):
        for level in range(LEVELS, 0, -1):

            def pull(base, level=level, which=which):
                index = column_index(base, level)
                count = rows + 2 * level
                shift = REACH - level - 1
                spread_sums = rows_box(spreads[which * LEVELS + level - 1], base, shift, shift, count, first, last)
                if level < LEVELS:
                    grown_sums = rows_box(parts[which * LEVELS + level], base, 0, 0, count, first, last)
                for x in range(count):
                    ok = index < column_limit(x, level)
                    spread = next(spread_sums)
                    grown = next(grown_sums) if level < LEVELS else None
                    for h in range(2):
                        off = WIDE - 2 * level
                        inv = inverses[level - 1][x + off, h, pl.ds(base + off, SUBLANES), :]
                        part = -(inv * spread[h])
                        if level < LEVELS:
                            at = REACH - level
                            own = weights[level][x + at, h, pl.ds(base + at, SUBLANES), :]
                            if which:
                                own = own * labels[x + at, h, pl.ds(base + at, SUBLANES), :]
                            part = (part + own) * inv + grown[h]
                        else:
                            part = part * inv
                        parts[which * LEVELS + level - 1][x, h, pl.ds(base, SUBLANES), :] = jnp.where(ok, part, 0.0)

            over_tiles(cols + 2 * level, pull)

        def finish(base, which=which):
            grown_sums = rows_box(parts[which * LEVELS], base, 0, 0, rows, first, last)
            for x, grown in enumerate(grown_sums):
                for h in range(2):
                    power = powers[0][x + WIDE, h, pl.ds(base + WIDE, SUBLANES), :]
                    own = weights[0][x + REACH, h, pl.ds(base + REACH, SUBLANES), :]
                    if which:
                        own = own * labels[x + REACH, h, pl.ds(base + REACH, SUBLANES), :]
                    stage[1 - which, x, pl.ds(base, SUBLANES), h * LANES : (h + 1) * LANES] = power * grown[h] + own

        over_tiles(cols, finish)
        copies[1 - which].start()

    for copy in copies:
        copy.wait()


def combine_kernel(cells, got, results, gradient, loss):
    total = jnp.zeros((SUBLANES, LANES), jnp.float32)
    for i in range(got.shape[0] // SUBLANES):
        total += got[i * SUBLANES : (i + 1) * SUBLANES, :]
    total = total + pltpu.roll(total, 4, 0)
    total = jnp.broadcast_to(jnp.sum(total, 1, keepdims=True), (SUBLANES, LANES))
    intersection_pred, mass_pred, intersection_mask, mass_mask = (total[i : i + 1] + 1.0 for i in range(4))
    precision = intersection_pred / mass_pred
    sensitivity = intersection_mask / mass_mask
    paired = precision + sensitivity
    loss[0] = jnp.max(1.0 - 2.0 * precision * sensitivity / paired)
    slope_prec = -2.0 * sensitivity * sensitivity / (paired * paired)
    slope_sens = -2.0 * precision * precision / (paired * paired)
    coef_intersection = cells * slope_prec / mass_pred
    coef_mass = -coef_intersection * precision
    coef_cross = cells * slope_sens / mass_mask
    a, b, c = (
        jnp.broadcast_to(jnp.concatenate([v, v], 1), (gradient.shape[1], 2 * LANES))
        for v in (coef_intersection, coef_mass, coef_cross)
    )
    for x in range(gradient.shape[0]):
        gradient[x] = a * results[0, x] + b * results[1, x] + c * results[2, x]


def local(prediction, vessel_mask):
    rows, cols, depth = prediction.shape
    none = (0, 0)
    packed = lax.optimization_barrier(
        jnp.pad(prediction, ((0, rows), none, none)) + jnp.pad(vessel_mask, ((rows, 0), none, none)).astype(jnp.float32)
    )
    gx, gy = lax.axis_size("gx"), lax.axis_size("gy")
    place = jnp.stack(
        [lax.axis_index("gx") * rows, lax.axis_index("gy") * cols, jnp.int32(gx * rows), jnp.int32(gy * cols)]
    ).astype(jnp.int32)
    pred_ext, mask_ext = with_halo(packed, rows)

    def held(width, margin=2):
        return pltpu.VMEM((rows + 2 * width, 2, tiles_for(cols + 2 * width + margin + 6) * SUBLANES, LANES), jnp.float32)

    scratch = (
        [held(WIDE - k) for k in range(LEVELS + 1)]
        + [held(WIDE - k) for k in range(1, LEVELS + 1)]
        + [held(REACH)] * 4
        + [held(REACH)] * 4
        + [held(REACH)] * 8
        + [held(k) for k in range(1, LEVELS + 1)] * 2
        + [held(REACH)] * 2
        + [held(REACH - k) for k in range(LEVELS + 1)]
        + [held(REACH - k) for k in range(1, LEVELS + 1)]
        + [held(0)] * 4
        + [pltpu.VMEM((3, rows, cols, depth), jnp.float32), pltpu.VMEM((gx * gy * 4, LANES), jnp.float32), pltpu.SemaphoreType.DMA((4,))]
    )
    block = jax.ShapeDtypeStruct((rows, cols, depth), jnp.float32)
    vmem = pl.BlockSpec(memory_space=pltpu.VMEM)
    smem = pl.BlockSpec(memory_space=pltpu.SMEM)
    results, sums = pl.pallas_call(
        lambda *refs: skeleton_kernel(rows, cols, *refs),
        out_shape=[jax.ShapeDtypeStruct((3, rows, cols, depth), jnp.float32), jax.ShapeDtypeStruct((gx * gy * 4, LANES), jnp.float32)],
        in_specs=[smem, vmem, vmem, vmem],
        out_specs=[pl.BlockSpec(memory_space=pltpu.HBM)] * 2,
        scratch_shapes=scratch,
        compiler_params=pltpu.CompilerParams(vmem_limit_bytes=VMEM_BYTES),
        name="skeleton",
    )(place, packed[:rows], pred_ext, mask_ext)
    got = lax.all_to_all(sums, ("gx", "gy"), 0, 0, tiled=True)
    gradient, loss = pl.pallas_call(
        lambda *refs: combine_kernel(float(gx * rows * gy * cols * depth), *refs),
        out_shape=[block, jax.ShapeDtypeStruct((1,), jnp.float32)],
        in_specs=[vmem] * 2,
        out_specs=[vmem, smem],
        name="combine",
    )(got, results)
    return (gradient, loss[0])


def solution(mesh):
    placed = (P("gx", "gy", None), P("gx", "gy", None))
    return jax.shard_map(
        local, mesh=mesh, in_specs=placed, out_specs=(P("gx", "gy", None), P()), check_vma=False
    )
```

```python
import jax
import jax.numpy as jnp
from jax import lax
from jax.experimental import pallas as pl
from jax.experimental.pallas import tpu as pltpu
from jax.sharding import PartitionSpec as P

ITERS = 3
LEVELS = ITERS + 1
REACH = LEVELS + 1
softness_factor = 0.1


def moved(block, axis, target):
    count = lax.axis_size(axis)
    pairs = [(i, target(i)) for i in range(count) if 0 <= target(i) < count]
    return lax.ppermute(block, axis, pairs)


def with_halo(packed, rows):
    wide, thin = 2 * REACH, REACH
    rest = wide - rows
    own_pred, own_mask = packed[:rows], packed[rows:]
    spot = lax.axis_index("gx")
    odd, upper = lax.rem(spot, 2) == 1, lax.rem(spot, 4) >= 2
    to_up = jnp.concatenate([own_pred, own_mask[rows - thin :]], 0)
    to_down = jnp.concatenate([own_pred, own_mask[:thin]], 0)
    to_far_up, to_far_down = own_pred[rows - rest :], own_pred[:rest]
    a, b, c, d = lax.optimization_barrier(
        (
            jnp.where(odd, to_down, to_up),
            jnp.where(odd, to_up, to_down),
            jnp.where(upper, to_far_down, to_far_up),
            jnp.where(upper, to_far_up, to_far_down),
        )
    )
    a = moved(a, "gx", lambda i: i ^ 1)
    b = moved(b, "gx", lambda i: i + 1 if i % 2 else i - 1)
    c = moved(c, "gx", lambda i: i ^ 2)
    d = moved(d, "gx", lambda i: i + 2 if i % 4 >= 2 else i - 2)
    a, b, c, d = lax.optimization_barrier((a, b, c, d))
    up, down = jnp.where(odd, a, b), jnp.where(odd, b, a)
    far_up, far_down = jnp.where(upper, c, d), jnp.where(upper, d, c)
    tall_pred = jnp.concatenate([far_up, up[:rows], own_pred, down[:rows], far_down], 0)
    tall_mask = jnp.concatenate([up[rows:], own_mask, down[rows:]], 0)
    tall, short = tall_pred.shape[0], tall_mask.shape[0]

    def side(p, m):
        return jnp.concatenate([p.reshape(tall * wide, -1), m.reshape(short * thin, -1)], 0)

    def unside(b):
        return b[: tall * wide].reshape(tall, wide, -1), b[tall * wide :].reshape(short, thin, -1)

    col_odd = lax.rem(lax.axis_index("gy"), 2) == 1
    high = side(tall_pred[:, -wide:], tall_mask[:, -thin:])
    low = side(tall_pred[:, :wide], tall_mask[:, :thin])
    first = moved(jnp.where(col_odd, low, high), "gy", lambda i: i ^ 1)
    second = moved(jnp.where(col_odd, high, low), "gy", lambda i: i + 1 if i % 2 else i - 1)
    first, second = lax.optimization_barrier((first, second))
    left_pred, left_mask = unside(jnp.where(col_odd, first, second))
    right_pred, right_mask = unside(jnp.where(col_odd, second, first))

    def framed(parts):
        count = sum(p.shape[1] for p in parts)
        return jnp.pad(jnp.concatenate(parts, 1), ((0, 0), (0, tiles_for(count) * SUBLANES - count), (0, 0)))

    return framed([left_pred, tall_pred, right_pred]), framed([left_mask, tall_mask, right_mask])


WIDE = 2 * REACH
LANES = 128
SUBLANES = 8
VMEM_BYTES = 40 * 1024 * 1024
KEPT = 210


def tiles_for(count):
    return -(-count // SUBLANES)


def depth_sum(low, high, first, last):
    low_up, high_up = pltpu.roll(low, 1, 1), pltpu.roll(high, 1, 1)
    low_down, high_down = pltpu.roll(low, LANES - 1, 1), pltpu.roll(high, LANES - 1, 1)
    return (
        low + jnp.where(first, 0.0, low_up) + jnp.where(last, high_down, low_down),
        high + jnp.where(first, low_up, high_up) + jnp.where(last, 0.0, high_down),
    )


def rows_box(ref, base, row_shift, col_shift, count, first, last):
    def across(x, h):
        parts = [ref[x + row_shift, h, pl.ds(base + (col_shift + d), SUBLANES), :] for d in range(3)]
        return parts[0] + parts[1] + parts[2]

    older = [across(0, h) for h in range(2)]
    newer = [across(1, h) for h in range(2)]
    for x in range(count):
        newest = [across(x + 2, h) for h in range(2)]
        low, high = (older[h] + newer[h] + newest[h] for h in range(2))
        older, newer = newer, newest
        yield depth_sum(low, high, first, last)


def over_tiles(count, step):
    def body(i, carry):
        step(i * SUBLANES)
        return carry

    lax.fori_loop(0, tiles_for(count), body, 0, unroll=True)


def skeleton_kernel(rows, cols, place, own_pred, pred, label, results, sums, *scratch):
    t = softness_factor
    scratch = list(scratch)
    stage, sent, copied = scratch[48:]
    mask_skel = stage.at[2]
    tiles = [pl.ds(base, SUBLANES) for base in range(0, cols, SUBLANES)]
    copies = [
        [pltpu.make_async_copy(stage.at[i, :, t], results.at[i, :, t], copied.at[i, n]) for n, t in enumerate(tiles)]
        for i in range(3)
    ]
    copies.append([pltpu.make_async_copy(sent, sums, copied.at[3, 0])])
    powers = scratch[:5]
    inverses = scratch[5:9]
    opened = scratch[9:13]
    weights = scratch[13:17]
    spreads = scratch[17:25]
    parts = scratch[25:33]
    labels, skels = scratch[33:35]
    label_powers = scratch[35:40]
    label_inverses = scratch[40:44]
    label_opened = scratch[44:48]
    row0, col0, row_count, col_count = (place[i] for i in range(4))
    lane = lax.broadcasted_iota(jnp.int32, (SUBLANES, LANES), 1)
    sublane = lax.broadcasted_iota(jnp.int32, (SUBLANES, LANES), 0)
    first, last = lane == 0, lane == LANES - 1

    def column_index(base, width):
        index = sublane + (base + (col0 - width))
        return jnp.where(index < 0, 1 << 20, index)

    def column_limit(x, width):
        row = row0 + (x - width)
        return jnp.where((row >= 0) & (row < row_count), col_count, 0)

    def raise_field(field, powers, inverses, width):
        def start(base):
            index = column_index(base, width)
            for x in range(rows + 2 * width):
                ok = index < column_limit(x, width)
                for h in range(2):
                    value = field[x, pl.ds(base, SUBLANES), h * LANES : (h + 1) * LANES]
                    powers[0][x, h, pl.ds(base, SUBLANES), :] = jnp.where(ok, jnp.exp(value * (-1.0 / t)), 0.0)

        over_tiles(cols + 2 * width, start)
        for level in range(1, LEVELS + 1):
            here = width - level

            def erode(base, level=level, here=here):
                index = column_index(base, here)
                sums_of = rows_box(powers[level - 1], base, 0, 0, rows + 2 * here, first, last)
                for x, pair in enumerate(sums_of):
                    ok = index < column_limit(x, here)
                    for h in range(2):
                        powers[level][x, h, pl.ds(base, SUBLANES), :] = jnp.where(ok, pair[h], 0.0)
                        inverses[level - 1][x, h, pl.ds(base, SUBLANES), :] = jnp.where(ok, 1.0 / pair[h], 0.0)

            over_tiles(cols + 2 * here, erode)

    def open_field(inverses, opened, width, keep):
        for level in range(1, LEVELS + 1):
            shift = width - level - keep - 1

            def dilate(base, level=level, shift=shift):
                sums_of = rows_box(inverses[level - 1], base, shift, shift, rows + 2 * keep, first, last)
                for x, pair in enumerate(sums_of):
                    for h in range(2):
                        opened[level - 1][x, h, pl.ds(base, SUBLANES), :] = pair[h]

            over_tiles(cols + 2 * keep, dilate)

    def chain(power_of, opened_of):
        skel, saved = None, []
        for j in range(LEVELS):
            wide = opened_of(j)
            product = power_of(j) * wide
            over = 1.0 / (wide * (1.0 + product))
            slope = wide * over
            delta = -jnp.log(product * slope)
            if skel is None:
                skel = delta
                saved.append((slope, over, delta, None, None))
            else:
                left = 1.0 - t * skel
                e = jnp.exp(delta * left)
                grown = 1.0 + e
                saved.append((slope, over, delta, left, e / grown))
                skel = skel + jnp.log(grown)
        return skel, saved

    raise_field(label, label_powers, label_inverses, REACH)
    open_field(label_inverses, label_opened, REACH, 0)

    def label_chain(base):
        for x in range(rows):
            for h in range(2):
                skel, _ = chain(
                    lambda j: label_powers[j][x + REACH - j, h, pl.ds(base + (REACH - j), SUBLANES), :],
                    lambda j: label_opened[j][x, h, pl.ds(base, SUBLANES), :],
                )
                mask_skel[x, pl.ds(base, SUBLANES), h * LANES : (h + 1) * LANES] = t * skel

    over_tiles(cols, label_chain)
    for copy in copies[2]:
        copy.start()

    def spread_label(base):
        for x in range(rows + 2 * REACH):
            for h in range(2):
                labels[x, h, pl.ds(base, SUBLANES), :] = label[x, pl.ds(base, SUBLANES), h * LANES : (h + 1) * LANES]

    over_tiles(cols + 2 * REACH, spread_label)

    raise_field(pred, powers, inverses, WIDE)
    open_field(inverses, opened, WIDE, REACH)

    chunk = 3

    def chain_chunk(base, x0):
        index = column_index(base, REACH)
        for dx in range(chunk):
            x = x0 + dx
            ok = index < column_limit(x, REACH)
            for h in range(2):
                skel, saved = chain(
                    lambda j: powers[j][x + REACH - j, h, pl.ds(base + (REACH - j), SUBLANES), :],
                    lambda j: opened[j][x, h, pl.ds(base, SUBLANES), :],
                )
                skels[x, h, pl.ds(base, SUBLANES), :] = t * skel
                seed = labels[x, h, pl.ds(base, SUBLANES), :]
                rest = jnp.where(ok, 1.0, 0.0)
                for j in range(ITERS, -1, -1):
                    slope, over, delta, left, rect = saved[j]
                    if j:
                        inner = rest * rect
                        scaled = inner * left
                        rest = rest - inner * (t * delta)
                    else:
                        scaled = rest
                    weights[j][x, h, pl.ds(base, SUBLANES), :] = jnp.where(ok, scaled * slope, 0.0)
                    spread = jnp.where(ok, scaled * over, 0.0)
                    spreads[j][x, h, pl.ds(base, SUBLANES), :] = spread
                    spreads[LEVELS + j][x, h, pl.ds(base, SUBLANES), :] = seed * spread

    def chain_tile(base):
        def body(i, carry):
            chain_chunk(base, i * chunk)
            return carry

        lax.fori_loop(0, (rows + 2 * REACH) // chunk, body, 0, unroll=True)

    over_tiles(cols + 2 * REACH, chain_tile)

    totals = [jnp.zeros((SUBLANES, LANES), jnp.float32) for _ in range(4)]
    for base in range(0, cols, SUBLANES):
        for x in range(rows):
            for h in range(2):
                half = slice(h * LANES, (h + 1) * LANES)
                skel = skels[x + REACH, h, pl.ds(base + REACH, SUBLANES), :]
                other = mask_skel[x, pl.ds(base, SUBLANES), half]
                totals[0] += skel * labels[x + REACH, h, pl.ds(base + REACH, SUBLANES), :]
                totals[1] += skel
                totals[2] += other * own_pred[x, pl.ds(base, SUBLANES), half]
                totals[3] += other
    totals = [jnp.sum(jnp.sum(v, 0, keepdims=True), 1, keepdims=True) for v in totals]
    packed = jnp.broadcast_to(jnp.concatenate(totals * 2, 0), (SUBLANES, LANES))
    for i in range(sums.shape[0] // SUBLANES):
        sent[i * SUBLANES : (i + 1) * SUBLANES, :] = packed
    copies[3][0].start()

    for which in range(2):
        for level in range(LEVELS, 0, -1):

            def pull(base, level=level, which=which):
                index = column_index(base, level)
                count = rows + 2 * level
                shift = REACH - level - 1
                spread_sums = rows_box(spreads[which * LEVELS + level - 1], base, shift, shift, count, first, last)
                if level < LEVELS:
                    grown_sums = rows_box(parts[which * LEVELS + level], base, 0, 0, count, first, last)
                for x in range(count):
                    ok = index < column_limit(x, level)
                    spread = next(spread_sums)
                    grown = next(grown_sums) if level < LEVELS else None
                    for h in range(2):
                        off = WIDE - 2 * level
                        inv = inverses[level - 1][x + off, h, pl.ds(base + off, SUBLANES), :]
                        part = -(inv * spread[h])
                        if level < LEVELS:
                            at = REACH - level
                            own = weights[level][x + at, h, pl.ds(base + at, SUBLANES), :]
                            if which:
                                own = own * labels[x + at, h, pl.ds(base + at, SUBLANES), :]
                            part = (part + own) * inv + grown[h]
                        else:
                            part = part * inv
                        parts[which * LEVELS + level - 1][x, h, pl.ds(base, SUBLANES), :] = jnp.where(ok, part, 0.0)

            over_tiles(cols + 2 * level, pull)

        def finish(base, which=which):
            grown_sums = rows_box(parts[which * LEVELS], base, 0, 0, rows, first, last)
            for x, grown in enumerate(grown_sums):
                for h in range(2):
                    power = powers[0][x + WIDE, h, pl.ds(base + WIDE, SUBLANES), :]
                    own = weights[0][x + REACH, h, pl.ds(base + REACH, SUBLANES), :]
                    if which:
                        own = own * labels[x + REACH, h, pl.ds(base + REACH, SUBLANES), :]
                    stage[1 - which, x, pl.ds(base, SUBLANES), h * LANES : (h + 1) * LANES] = power * grown[h] + own

        for tile in range(tiles_for(cols)):
            finish(tile * SUBLANES)
            copies[1 - which][tile].start()

    for copy in sum(copies, []):
        copy.wait()


def combine_kernel(cells, got, results, gradient, loss):
    total = jnp.zeros((SUBLANES, LANES), jnp.float32)
    for i in range(got.shape[0] // SUBLANES):
        total += got[i * SUBLANES : (i + 1) * SUBLANES, :]
    total = total + pltpu.roll(total, 4, 0)
    intersection_pred, mass_pred, intersection_mask, mass_mask = (total[i : i + 1] + 1.0 for i in range(4))
    precision = intersection_pred / mass_pred
    sensitivity = intersection_mask / mass_mask
    paired = precision + sensitivity
    loss[0] = (1.0 - 2.0 * precision * sensitivity / paired)[0, 0]
    slope_prec = -2.0 * sensitivity * sensitivity / (paired * paired)
    slope_sens = -2.0 * precision * precision / (paired * paired)
    coef_intersection = cells * slope_prec / mass_pred
    coef_mass = -coef_intersection * precision
    coef_cross = cells * slope_sens / mass_mask
    a, b, c = (
        jnp.broadcast_to(jnp.concatenate([v, v], 1), (gradient.shape[1], 2 * LANES))
        for v in (coef_intersection, coef_mass, coef_cross)
    )
    for x in range(gradient.shape[0]):
        gradient[x] = a * results[0, x] + b * results[1, x] + c * results[2, x]


def local(prediction, vessel_mask):
    rows, cols, depth = prediction.shape
    none = (0, 0)
    packed = lax.optimization_barrier(
        jnp.pad(prediction, ((0, rows), none, none)) + jnp.pad(vessel_mask, ((rows, 0), none, none)).astype(jnp.float32)
    )
    gx, gy = lax.axis_size("gx"), lax.axis_size("gy")
    place = jnp.stack(
        [lax.axis_index("gx") * rows, lax.axis_index("gy") * cols, jnp.int32(gx * rows), jnp.int32(gy * cols)]
    ).astype(jnp.int32)
    pred_ext, mask_ext = with_halo(packed, rows)

    def held(width, margin=2):
        return pltpu.VMEM((rows + 2 * width, 2, tiles_for(cols + 2 * width + margin + 6) * SUBLANES, LANES), jnp.float32)

    scratch = (
        [held(WIDE - k) for k in range(LEVELS + 1)]
        + [held(WIDE - k) for k in range(1, LEVELS + 1)]
        + [held(REACH)] * 4
        + [held(REACH)] * 4
        + [held(REACH)] * 8
        + [held(k) for k in range(1, LEVELS + 1)] * 2
        + [held(REACH)] * 2
        + [held(REACH - k) for k in range(LEVELS + 1)]
        + [held(REACH - k) for k in range(1, LEVELS + 1)]
        + [held(0)] * 4
        + [pltpu.VMEM((3, rows, cols, depth), jnp.float32), pltpu.VMEM((gx * gy * 4, LANES), jnp.float32), pltpu.SemaphoreType.DMA((4, tiles_for(cols)))]
    )
    block = jax.ShapeDtypeStruct((rows, cols, depth), jnp.float32)
    vmem = pl.BlockSpec(memory_space=pltpu.VMEM)
    smem = pl.BlockSpec(memory_space=pltpu.SMEM)
    results, sums = pl.pallas_call(
        lambda *refs: skeleton_kernel(rows, cols, *refs),
        out_shape=[jax.ShapeDtypeStruct((KEPT, rows, cols, depth), jnp.float32), jax.ShapeDtypeStruct((gx * gy * 4, LANES), jnp.float32)],
        in_specs=[smem, vmem, vmem, vmem],
        out_specs=[pl.BlockSpec(memory_space=pltpu.HBM)] * 2,
        scratch_shapes=scratch,
        compiler_params=pltpu.CompilerParams(vmem_limit_bytes=VMEM_BYTES),
        name="skeleton",
    )(place, packed[:rows], pred_ext, mask_ext)
    got = lax.all_to_all(sums, ("gx", "gy"), 0, 0, tiled=True)
    gradient, loss = pl.pallas_call(
        lambda *refs: combine_kernel(float(gx * rows * gy * cols * depth), *refs),
        out_shape=[block, jax.ShapeDtypeStruct((1,), jnp.float32)],
        grid=(1,),
        in_specs=[
            pl.BlockSpec(got.shape, lambda i: (0, 0)),
            pl.BlockSpec((3, rows, cols, depth), lambda i: (0, 0, 0, 0)),
        ],
        out_specs=[pl.BlockSpec(block.shape, lambda i: (0, 0, 0)), smem],
        name="combine",
    )(got, results)
    return (gradient, loss[0])


def solution(mesh):
    placed = (P("gx", "gy", None), P("gx", "gy", None))
    return jax.shard_map(
        local, mesh=mesh, in_specs=placed, out_specs=(P("gx", "gy", None), P()), check_vma=False
    )
```

```python
import jax
import jax.numpy as jnp
from jax import lax
from jax.experimental import pallas as pl
from jax.experimental.pallas import tpu as pltpu
from jax.sharding import PartitionSpec as P

ITERS = 3
LEVELS = ITERS + 1
REACH = LEVELS + 1
softness_factor = 0.1


def moved(block, axis, target):
    count = lax.axis_size(axis)
    pairs = [(i, target(i)) for i in range(count) if 0 <= target(i) < count]
    return lax.ppermute(block, axis, pairs)


def with_halo(packed, rows):
    wide, thin = 2 * REACH, REACH
    rest = wide - rows
    own_pred, own_mask = packed[:rows], packed[rows:]
    spot = lax.axis_index("gx")
    odd, upper = lax.rem(spot, 2) == 1, lax.rem(spot, 4) >= 2
    to_up = jnp.concatenate([own_pred, own_mask[rows - thin :]], 0)
    to_down = jnp.concatenate([own_pred, own_mask[:thin]], 0)
    to_far_up, to_far_down = own_pred[rows - rest :], own_pred[:rest]
    a, b, c, d = lax.optimization_barrier(
        (
            jnp.where(odd, to_down, to_up),
            jnp.where(odd, to_up, to_down),
            jnp.where(upper, to_far_down, to_far_up),
            jnp.where(upper, to_far_up, to_far_down),
        )
    )
    a = moved(a, "gx", lambda i: i ^ 1)
    b = moved(b, "gx", lambda i: i + 1 if i % 2 else i - 1)
    c = moved(c, "gx", lambda i: i ^ 2)
    d = moved(d, "gx", lambda i: i + 2 if i % 4 >= 2 else i - 2)
    a, b, c, d = lax.optimization_barrier((a, b, c, d))
    up, down = jnp.where(odd, a, b), jnp.where(odd, b, a)
    far_up, far_down = jnp.where(upper, c, d), jnp.where(upper, d, c)
    tall_pred = jnp.concatenate([far_up, up[:rows], own_pred, down[:rows], far_down], 0)
    tall_mask = jnp.concatenate([up[rows:], own_mask, down[rows:]], 0)
    tall, short = tall_pred.shape[0], tall_mask.shape[0]

    def side(p, m):
        return jnp.concatenate([p.reshape(tall * wide, -1), m.reshape(short * thin, -1)], 0)

    def unside(b):
        return b[: tall * wide].reshape(tall, wide, -1), b[tall * wide :].reshape(short, thin, -1)

    col_odd = lax.rem(lax.axis_index("gy"), 2) == 1
    high = side(tall_pred[:, -wide:], tall_mask[:, -thin:])
    low = side(tall_pred[:, :wide], tall_mask[:, :thin])
    first = moved(jnp.where(col_odd, low, high), "gy", lambda i: i ^ 1)
    second = moved(jnp.where(col_odd, high, low), "gy", lambda i: i + 1 if i % 2 else i - 1)
    first, second = lax.optimization_barrier((first, second))
    left_pred, left_mask = unside(jnp.where(col_odd, first, second))
    right_pred, right_mask = unside(jnp.where(col_odd, second, first))

    def framed(parts):
        count = sum(p.shape[1] for p in parts)
        return jnp.pad(jnp.concatenate(parts, 1), ((0, 0), (0, tiles_for(count) * SUBLANES - count), (0, 0)))

    return framed([left_pred, tall_pred, right_pred]), framed([left_mask, tall_mask, right_mask])


WIDE = 2 * REACH
LANES = 128
SUBLANES = 8
VMEM_BYTES = 40 * 1024 * 1024
KEPT = 210


def tiles_for(count):
    return -(-count // SUBLANES)


def depth_sum(low, high, first, last):
    low_up, high_up = pltpu.roll(low, 1, 1), pltpu.roll(high, 1, 1)
    low_down, high_down = pltpu.roll(low, LANES - 1, 1), pltpu.roll(high, LANES - 1, 1)
    return (
        low + jnp.where(first, 0.0, low_up) + jnp.where(last, high_down, low_down),
        high + jnp.where(first, low_up, high_up) + jnp.where(last, 0.0, high_down),
    )


def rows_box(ref, base, row_shift, col_shift, count, first, last):
    def across(x, h):
        parts = [ref[x + row_shift, h, pl.ds(base + (col_shift + d), SUBLANES), :] for d in range(3)]
        return parts[0] + parts[1] + parts[2]

    rows = [[across(x, h) for h in range(2)] for x in range(2)]
    for x in range(0, count, 2):
        rows += [[across(x + d, h) for h in range(2)] for d in (2, 3)]
        shared = [rows[1][h] + rows[2][h] for h in range(2)]
        yield depth_sum(*(rows[0][h] + shared[h] for h in range(2)), first, last)
        yield depth_sum(*(shared[h] + rows[3][h] for h in range(2)), first, last)
        rows = rows[2:]


def over_tiles(count, step):
    def body(i, carry):
        step(i * SUBLANES)
        return carry

    lax.fori_loop(0, tiles_for(count), body, 0, unroll=True)


def skeleton_kernel(rows, cols, own_pred, pred, label, results, sums, *scratch):
    t = softness_factor
    scratch = list(scratch)
    stage, copied = scratch[48:]
    mask_skel = stage.at[2]
    tiles = [pl.ds(base, SUBLANES) for base in range(0, cols, SUBLANES)]
    copies = [
        [pltpu.make_async_copy(stage.at[i, :, t], results.at[i, :, t], copied.at[i, n]) for n, t in enumerate(tiles)]
        for i in range(3)
    ]
    powers = scratch[:5]
    inverses = scratch[5:9]
    opened = scratch[9:13]
    weights = scratch[13:17]
    spreads = scratch[17:25]
    parts = scratch[25:33]
    labels, skels = scratch[33:35]
    label_powers = scratch[35:40]
    label_inverses = scratch[40:44]
    label_opened = scratch[44:48]
    row0, row_count = lax.axis_index("gx") * rows, lax.axis_size("gx") * rows
    col0, col_count = lax.axis_index("gy") * cols, lax.axis_size("gy") * cols
    lane = lax.broadcasted_iota(jnp.int32, (SUBLANES, LANES), 1)
    sublane = lax.broadcasted_iota(jnp.int32, (SUBLANES, LANES), 0)
    first, last = lane == 0, lane == LANES - 1

    def column_index(base, width):
        index = sublane + (base + (col0 - width))
        return jnp.where(index < 0, 1 << 20, index)

    def column_limit(x, width):
        row = row0 + (x - width)
        return jnp.where((row >= 0) & (row < row_count), col_count, 0)

    def raise_field(field, powers, inverses, width, kept=None):
        def start(base):
            index = column_index(base, width)
            for x in range(rows + 2 * width):
                ok = index < column_limit(x, width)
                for h in range(2):
                    value = field[x, pl.ds(base, SUBLANES), h * LANES : (h + 1) * LANES]
                    if kept is not None:
                        kept[x, h, pl.ds(base, SUBLANES), :] = value
                    powers[0][x, h, pl.ds(base, SUBLANES), :] = jnp.where(ok, jnp.exp(value * (-1.0 / t)), 0.0)

        over_tiles(cols + 2 * width, start)
        for level in range(1, LEVELS + 1):
            here = width - level

            def erode(base, level=level, here=here):
                index = column_index(base, here)
                sums_of = rows_box(powers[level - 1], base, 0, 0, rows + 2 * here, first, last)
                for x, pair in enumerate(sums_of):
                    ok = index < column_limit(x, here)
                    for h in range(2):
                        if level < LEVELS:
                            powers[level][x, h, pl.ds(base, SUBLANES), :] = jnp.where(ok, pair[h], 0.0)
                        inverses[level - 1][x, h, pl.ds(base, SUBLANES), :] = jnp.where(ok, 1.0 / pair[h], 0.0)

            over_tiles(cols + 2 * here, erode)

    def open_field(inverses, opened, width, keep):
        for level in range(1, LEVELS + 1):
            shift = width - level - keep - 1

            def dilate(base, level=level, shift=shift):
                sums_of = rows_box(inverses[level - 1], base, shift, shift, rows + 2 * keep, first, last)
                for x, pair in enumerate(sums_of):
                    for h in range(2):
                        opened[level - 1][x, h, pl.ds(base, SUBLANES), :] = pair[h]

            over_tiles(cols + 2 * keep, dilate)

    def chain(power_of, opened_of):
        skel, saved = None, []
        for j in range(LEVELS):
            wide = opened_of(j)
            product = power_of(j) * wide
            over = 1.0 / (wide * (1.0 + product))
            slope = wide * over
            delta = -jnp.log(product * slope)
            if skel is None:
                skel = delta
                saved.append((slope, over, delta, None, None))
            else:
                left = 1.0 - t * skel
                e = jnp.exp(delta * left)
                grown = 1.0 + e
                saved.append((slope, over, delta, left, e / grown))
                skel = skel + jnp.log(grown)
        return skel, saved

    raise_field(label, label_powers, label_inverses, REACH, labels)
    open_field(label_inverses, label_opened, REACH, 0)

    def label_chain(base):
        for x in range(rows):
            for h in range(2):
                skel, _ = chain(
                    lambda j: label_powers[j][x + REACH - j, h, pl.ds(base + (REACH - j), SUBLANES), :],
                    lambda j: label_opened[j][x, h, pl.ds(base, SUBLANES), :],
                )
                mask_skel[x, pl.ds(base, SUBLANES), h * LANES : (h + 1) * LANES] = t * skel

    over_tiles(cols, label_chain)
    for copy in copies[2]:
        copy.start()

    raise_field(pred, powers, inverses, WIDE)
    open_field(inverses, opened, WIDE, REACH)

    def chain_tile(base):
        index = column_index(base, REACH)
        for x in range(rows + 2 * REACH):
            away = max(REACH - x, x - REACH - rows + 1)
            ok = index < column_limit(x, REACH)
            for h in range(2):
                skel, saved = chain(
                    lambda j: powers[j][x + REACH - j, h, pl.ds(base + (REACH - j), SUBLANES), :],
                    lambda j: opened[j][x, h, pl.ds(base, SUBLANES), :],
                )
                if away <= 0:
                    skels[x, h, pl.ds(base, SUBLANES), :] = t * skel
                seed = labels[x, h, pl.ds(base, SUBLANES), :]
                rest = jnp.where(ok, 1.0, 0.0)
                for j in range(ITERS, max(0, away - 2) - 1, -1):
                    slope, over, delta, left, rect = saved[j]
                    if j:
                        inner = rest * rect
                        scaled = inner * left
                        rest = rest - inner * (t * delta)
                    else:
                        scaled = rest
                    if away <= j:
                        weights[j][x, h, pl.ds(base, SUBLANES), :] = jnp.where(ok, scaled * slope, 0.0)
                    spread = jnp.where(ok, scaled * over, 0.0)
                    spreads[j][x, h, pl.ds(base, SUBLANES), :] = spread
                    spreads[LEVELS + j][x, h, pl.ds(base, SUBLANES), :] = seed * spread

    over_tiles(cols + 2 * REACH, chain_tile)

    for which in range(2):
        for level in range(LEVELS, 0, -1):

            def pull(base, level=level, which=which):
                index = column_index(base, level)
                count = rows + 2 * level
                shift = REACH - level - 1
                spread_sums = rows_box(spreads[which * LEVELS + level - 1], base, shift, shift, count, first, last)
                if level < LEVELS:
                    grown_sums = rows_box(parts[which * LEVELS + level], base, 0, 0, count, first, last)
                for x in range(count):
                    ok = index < column_limit(x, level)
                    spread = next(spread_sums)
                    grown = next(grown_sums) if level < LEVELS else None
                    for h in range(2):
                        off = WIDE - 2 * level
                        inv = inverses[level - 1][x + off, h, pl.ds(base + off, SUBLANES), :]
                        if level < LEVELS:
                            at = REACH - level
                            own = weights[level][x + at, h, pl.ds(base + at, SUBLANES), :]
                            if which:
                                own = own * labels[x + at, h, pl.ds(base + at, SUBLANES), :]
                            part = (own - inv * spread[h]) * inv + grown[h]
                        else:
                            part = inv * inv * -spread[h]
                        parts[which * LEVELS + level - 1][x, h, pl.ds(base, SUBLANES), :] = jnp.where(ok, part, 0.0)

            over_tiles(cols + 2 * level, pull)

        def finish(base, which=which):
            grown_sums = rows_box(parts[which * LEVELS], base, 0, 0, rows, first, last)
            for x, grown in enumerate(grown_sums):
                for h in range(2):
                    power = powers[0][x + WIDE, h, pl.ds(base + WIDE, SUBLANES), :]
                    own = weights[0][x + REACH, h, pl.ds(base + REACH, SUBLANES), :]
                    if which:
                        own = own * labels[x + REACH, h, pl.ds(base + REACH, SUBLANES), :]
                    stage[1 - which, x, pl.ds(base, SUBLANES), h * LANES : (h + 1) * LANES] = power * grown[h] + own

        for tile in range(tiles_for(cols)):
            finish(tile * SUBLANES)
            copies[1 - which][tile].start()

    totals = [jnp.zeros((SUBLANES, LANES), jnp.float32) for _ in range(4)]
    for base in range(0, cols, SUBLANES):
        for x in range(rows):
            for h in range(2):
                half = slice(h * LANES, (h + 1) * LANES)
                skel = skels[x + REACH, h, pl.ds(base + REACH, SUBLANES), :]
                other = mask_skel[x, pl.ds(base, SUBLANES), half]
                totals[0] += skel * labels[x + REACH, h, pl.ds(base + REACH, SUBLANES), :]
                totals[1] += skel
                totals[2] += other * own_pred[x, pl.ds(base, SUBLANES), half]
                totals[3] += other
    totals = [jnp.sum(jnp.sum(v, 0, keepdims=True), 1, keepdims=True) for v in totals]
    packed = jnp.broadcast_to(jnp.concatenate(totals * 2, 0), (SUBLANES, LANES))
    for i in range(sums.shape[0] // SUBLANES):
        sums[i * SUBLANES : (i + 1) * SUBLANES, :] = packed
    for copy in sum(copies, []):
        copy.wait()


def combine_kernel(cells, got, results, gradient, loss):
    total = jnp.zeros((SUBLANES, LANES), jnp.float32)
    for i in range(got.shape[0] // SUBLANES):
        total += got[i * SUBLANES : (i + 1) * SUBLANES, :]
    total = total + pltpu.roll(total, 4, 0)
    intersection_pred, mass_pred, intersection_mask, mass_mask = (total[i : i + 1] + 1.0 for i in range(4))
    precision = intersection_pred / mass_pred
    sensitivity = intersection_mask / mass_mask
    paired = precision + sensitivity
    loss[0] = (1.0 - 2.0 * precision * sensitivity / paired)[0, 0]
    slope_prec = -2.0 * sensitivity * sensitivity / (paired * paired)
    slope_sens = -2.0 * precision * precision / (paired * paired)
    coef_intersection = cells * slope_prec / mass_pred
    coef_mass = -coef_intersection * precision
    coef_cross = cells * slope_sens / mass_mask
    a, b, c = (
        jnp.broadcast_to(jnp.concatenate([v, v], 1), (gradient.shape[1], 2 * LANES))
        for v in (coef_intersection, coef_mass, coef_cross)
    )
    for x in range(gradient.shape[0]):
        gradient[x] = a * results[0, x] + b * results[1, x] + c * results[2, x]


def local(prediction, vessel_mask):
    rows, cols, depth = prediction.shape
    none = (0, 0)
    packed = lax.optimization_barrier(
        jnp.pad(prediction, ((0, rows), none, none)) + jnp.pad(vessel_mask, ((rows, 0), none, none)).astype(jnp.float32)
    )
    gx, gy = lax.axis_size("gx"), lax.axis_size("gy")
    pred_ext, mask_ext = with_halo(packed, rows)

    def held(width, margin=2):
        return pltpu.VMEM((rows + 2 * width, 2, tiles_for(cols + 2 * width + margin + 6) * SUBLANES, LANES), jnp.float32)

    scratch = (
        [held(WIDE - k) for k in range(LEVELS + 1)]
        + [held(WIDE - k) for k in range(1, LEVELS + 1)]
        + [held(REACH)] * 4
        + [held(REACH)] * 4
        + [held(REACH)] * 8
        + [held(k) for k in range(1, LEVELS + 1)] * 2
        + [held(REACH)] * 2
        + [held(REACH - k) for k in range(LEVELS + 1)]
        + [held(REACH - k) for k in range(1, LEVELS + 1)]
        + [held(0)] * 4
        + [pltpu.VMEM((3, rows, cols, depth), jnp.float32), pltpu.SemaphoreType.DMA((3, tiles_for(cols)))]
    )
    block = jax.ShapeDtypeStruct((rows, cols, depth), jnp.float32)
    vmem = pl.BlockSpec(memory_space=pltpu.VMEM)
    smem = pl.BlockSpec(memory_space=pltpu.SMEM)
    results, sums = pl.pallas_call(
        lambda *refs: skeleton_kernel(rows, cols, *refs),
        out_shape=[jax.ShapeDtypeStruct((KEPT, rows, cols, depth), jnp.float32), jax.ShapeDtypeStruct((gx * gy * 4, LANES), jnp.float32)],
        in_specs=[vmem, vmem, vmem],
        out_specs=[pl.BlockSpec(memory_space=pltpu.HBM), vmem],
        scratch_shapes=scratch,
        compiler_params=pltpu.CompilerParams(vmem_limit_bytes=VMEM_BYTES),
        name="skeleton",
    )(packed[:rows], pred_ext, mask_ext)
    got = lax.all_to_all(sums, ("gx", "gy"), 0, 0, tiled=True)
    gradient, loss = pl.pallas_call(
        lambda *refs: combine_kernel(float(gx * rows * gy * cols * depth), *refs),
        out_shape=[block, jax.ShapeDtypeStruct((1,), jnp.float32)],
        grid=(1,),
        in_specs=[
            pl.BlockSpec(got.shape, lambda i: (0, 0)),
            pl.BlockSpec((3, rows, cols, depth), lambda i: (0, 0, 0, 0)),
        ],
        out_specs=[pl.BlockSpec(block.shape, lambda i: (0, 0, 0)), smem],
        name="combine",
    )(got, results)
    return (gradient, loss[0])


def solution(mesh):
    placed = (P("gx", "gy", None), P("gx", "gy", None))
    return jax.shard_map(
        local, mesh=mesh, in_specs=placed, out_specs=(P("gx", "gy", None), P()), check_vma=False
    )
```

```python
import jax
import jax.numpy as jnp
from jax import lax
from jax.experimental import pallas as pl
from jax.experimental.pallas import tpu as pltpu
from jax.sharding import PartitionSpec as P

ITERS = 3
LEVELS = ITERS + 1
REACH = LEVELS + 1
softness_factor = 0.1


def moved(block, axis, target):
    count = lax.axis_size(axis)
    pairs = [(i, target(i)) for i in range(count) if 0 <= target(i) < count]
    return lax.ppermute(block, axis, pairs)


def with_halo(packed, rows):
    wide, thin = 2 * REACH, REACH
    rest = wide - rows
    own_pred, own_mask = packed[:rows], packed[rows:]
    spot = lax.axis_index("gx")
    odd, upper = lax.rem(spot, 2) == 1, lax.rem(spot, 4) >= 2
    to_up = jnp.concatenate([own_pred, own_mask[rows - thin :]], 0)
    to_down = jnp.concatenate([own_pred, own_mask[:thin]], 0)
    to_far_up, to_far_down = own_pred[rows - rest :], own_pred[:rest]
    a, b, c, d = lax.optimization_barrier(
        (
            jnp.where(odd, to_down, to_up),
            jnp.where(odd, to_up, to_down),
            jnp.where(upper, to_far_down, to_far_up),
            jnp.where(upper, to_far_up, to_far_down),
        )
    )
    a = moved(a, "gx", lambda i: i ^ 1)
    b = moved(b, "gx", lambda i: i + 1 if i % 2 else i - 1)
    c = moved(c, "gx", lambda i: i ^ 2)
    d = moved(d, "gx", lambda i: i + 2 if i % 4 >= 2 else i - 2)
    a, b, c, d = lax.optimization_barrier((a, b, c, d))
    up, down = jnp.where(odd, a, b), jnp.where(odd, b, a)
    far_up, far_down = jnp.where(upper, c, d), jnp.where(upper, d, c)
    tall_pred = jnp.concatenate([far_up, up[:rows], own_pred, down[:rows], far_down], 0)
    tall_mask = jnp.concatenate([up[rows:], own_mask, down[rows:]], 0)
    tall, short = tall_pred.shape[0], tall_mask.shape[0]

    def side(p, m):
        flat = jnp.concatenate([p.reshape(tall * wide, -1), m.reshape(short * thin, -1)], 0)
        return jnp.pad(flat, ((0, -flat.shape[0] % SUBLANES), (0, 0)))

    col_odd = lax.rem(lax.axis_index("gy"), 2) == 1
    high = side(tall_pred[:, -wide:], tall_mask[:, -thin:])
    low = side(tall_pred[:, :wide], tall_mask[:, :thin])
    first = moved(jnp.where(col_odd, low, high), "gy", lambda i: i ^ 1)
    second = moved(jnp.where(col_odd, high, low), "gy", lambda i: i + 1 if i % 2 else i - 1)
    first, second = lax.optimization_barrier((first, second))
    return tall_pred, tall_mask, jnp.where(col_odd, first, second), jnp.where(col_odd, second, first)


WIDE = 2 * REACH
LANES = 128
SUBLANES = 8
VMEM_BYTES = 40 * 1024 * 1024
KEPT = 210


def tiles_for(count):
    return -(-count // SUBLANES)


def depth_sum(low, high, first, last):
    low_up, high_up = pltpu.roll(low, 1, 1), pltpu.roll(high, 1, 1)
    low_down, high_down = pltpu.roll(low, LANES - 1, 1), pltpu.roll(high, LANES - 1, 1)
    return (
        low + jnp.where(first, 0.0, low_up) + jnp.where(last, high_down, low_down),
        high + jnp.where(first, low_up, high_up) + jnp.where(last, 0.0, high_down),
    )


def rows_box(ref, base, row_shift, col_shift, count, first, last):
    def across(x, h):
        parts = [ref[x + row_shift, h, pl.ds(base + (col_shift + d), SUBLANES), :] for d in range(3)]
        return parts[0] + parts[1] + parts[2]

    rows = [[across(x, h) for h in range(2)] for x in range(2)]
    for x in range(0, count, 2):
        rows += [[across(x + d, h) for h in range(2)] for d in (2, 3)]
        shared = [rows[1][h] + rows[2][h] for h in range(2)]
        yield depth_sum(*(rows[0][h] + shared[h] for h in range(2)), first, last)
        yield depth_sum(*(shared[h] + rows[3][h] for h in range(2)), first, last)
        rows = rows[2:]


def over_tiles(count, step):
    def body(i, carry):
        step(i * SUBLANES)
        return carry

    lax.fori_loop(0, tiles_for(count), body, 0, unroll=True)


def skeleton_kernel(rows, cols, own_pred, pred, label, left, right, results, sums, *scratch):
    t = softness_factor
    scratch = list(scratch)
    stage, copied = scratch[48:]
    mask_skel = stage.at[2]
    tiles = [pl.ds(base, SUBLANES) for base in range(0, cols, SUBLANES)]
    copies = [
        [pltpu.make_async_copy(stage.at[i, :, t], results.at[i, :, t], copied.at[i, n]) for n, t in enumerate(tiles)]
        for i in range(3)
    ]
    powers = scratch[:5]
    inverses = scratch[5:9]
    opened = scratch[9:13]
    weights = scratch[13:17]
    spreads = scratch[17:25]
    parts = scratch[25:33]
    labels, skels = scratch[33:35]
    label_powers = scratch[35:40]
    label_inverses = scratch[40:44]
    label_opened = scratch[44:48]
    row0, row_count = lax.axis_index("gx") * rows, lax.axis_size("gx") * rows
    col0, col_count = lax.axis_index("gy") * cols, lax.axis_size("gy") * cols
    lane = lax.broadcasted_iota(jnp.int32, (SUBLANES, LANES), 1)
    sublane = lax.broadcasted_iota(jnp.int32, (SUBLANES, LANES), 0)
    first, last = lane == 0, lane == LANES - 1

    def column_index(base, width):
        index = sublane + (base + (col0 - width))
        return jnp.where(index < 0, 1 << 20, index)

    def column_limit(x, width):
        row = row0 + (x - width)
        return jnp.where((row >= 0) & (row < row_count), col_count, 0)

    def raise_field(middle, offset, powers, inverses, width, kept=None):
        last_tile = max(width - SUBLANES, 0)
        sides = (0, last_tile) if last_tile else (0,)
        tiles = [(at, left, at) for at in sides]
        tiles += [(width + at, None, at) for at in range(0, cols, SUBLANES)]
        tiles += [(width + cols + at, right, at) for at in sides]
        indices = [column_index(base, width) for base, _, _ in tiles]
        for x in range(rows + 2 * width):
            limit = column_limit(x, width)
            for (base, source, at), index in zip(tiles, indices):
                ok = index < limit
                for h in range(2):
                    half = slice(h * LANES, (h + 1) * LANES)
                    if source is None:
                        value = middle[x, at : at + SUBLANES, half]
                    else:
                        row = offset + x * width + at
                        value = source[row : row + SUBLANES, half]
                    if kept is not None:
                        kept[x, h, pl.ds(base, SUBLANES), :] = value
                    powers[0][x, h, pl.ds(base, SUBLANES), :] = jnp.where(ok, jnp.exp(value * (-1.0 / t)), 0.0)

        for level in range(1, LEVELS + 1):
            here = width - level

            def erode(base, level=level, here=here):
                index = column_index(base, here)
                sums_of = rows_box(powers[level - 1], base, 0, 0, rows + 2 * here, first, last)
                for x, pair in enumerate(sums_of):
                    ok = index < column_limit(x, here)
                    for h in range(2):
                        if level < LEVELS:
                            powers[level][x, h, pl.ds(base, SUBLANES), :] = jnp.where(ok, pair[h], 0.0)
                        inverses[level - 1][x, h, pl.ds(base, SUBLANES), :] = jnp.where(ok, 1.0 / pair[h], 0.0)

            over_tiles(cols + 2 * here, erode)

    def open_field(inverses, opened, width, keep):
        for level in range(1, LEVELS + 1):
            shift = width - level - keep - 1

            def dilate(base, level=level, shift=shift):
                sums_of = rows_box(inverses[level - 1], base, shift, shift, rows + 2 * keep, first, last)
                for x, pair in enumerate(sums_of):
                    for h in range(2):
                        opened[level - 1][x, h, pl.ds(base, SUBLANES), :] = pair[h]

            over_tiles(cols + 2 * keep, dilate)

    def chain(power_of, opened_of):
        skel, saved = None, []
        for j in range(LEVELS):
            wide = opened_of(j)
            product = power_of(j) * wide
            over = 1.0 / (wide * (1.0 + product))
            slope = wide * over
            delta = -jnp.log(product * slope)
            if skel is None:
                skel = delta
                saved.append((slope, over, delta, None, None))
            else:
                left = 1.0 - t * skel
                e = jnp.exp(delta * left)
                grown = 1.0 + e
                saved.append((slope, over, delta, left, e / grown))
                skel = skel + jnp.log(grown)
        return skel, saved

    raise_field(label, (rows + 2 * WIDE) * WIDE, label_powers, label_inverses, REACH, labels)
    open_field(label_inverses, label_opened, REACH, 0)

    def label_chain(base):
        for x in range(rows):
            for h in range(2):
                skel, _ = chain(
                    lambda j: label_powers[j][x + REACH - j, h, pl.ds(base + (REACH - j), SUBLANES), :],
                    lambda j: label_opened[j][x, h, pl.ds(base, SUBLANES), :],
                )
                mask_skel[x, pl.ds(base, SUBLANES), h * LANES : (h + 1) * LANES] = t * skel

    over_tiles(cols, label_chain)
    for copy in copies[2]:
        copy.start()

    raise_field(pred, 0, powers, inverses, WIDE)
    open_field(inverses, opened, WIDE, REACH)

    def chain_tile(base):
        index = column_index(base, REACH)
        for x in range(rows + 2 * REACH):
            away = max(REACH - x, x - REACH - rows + 1)
            ok = index < column_limit(x, REACH)
            for h in range(2):
                skel, saved = chain(
                    lambda j: powers[j][x + REACH - j, h, pl.ds(base + (REACH - j), SUBLANES), :],
                    lambda j: opened[j][x, h, pl.ds(base, SUBLANES), :],
                )
                if away <= 0:
                    skels[x, h, pl.ds(base, SUBLANES), :] = t * skel
                seed = labels[x, h, pl.ds(base, SUBLANES), :]
                rest = jnp.where(ok, 1.0, 0.0)
                for j in range(ITERS, max(0, away - 2) - 1, -1):
                    slope, over, delta, left, rect = saved[j]
                    if j:
                        inner = rest * rect
                        scaled = inner * left
                        rest = rest - inner * (t * delta)
                    else:
                        scaled = rest
                    if away <= j:
                        weights[j][x, h, pl.ds(base, SUBLANES), :] = jnp.where(ok, scaled * slope, 0.0)
                    spread = jnp.where(ok, scaled * over, 0.0)
                    spreads[j][x, h, pl.ds(base, SUBLANES), :] = spread
                    spreads[LEVELS + j][x, h, pl.ds(base, SUBLANES), :] = seed * spread

    over_tiles(cols + 2 * REACH, chain_tile)

    for which in range(2):
        for level in range(LEVELS, 0, -1):

            def pull(base, level=level, which=which):
                index = column_index(base, level)
                count = rows + 2 * level
                shift = REACH - level - 1
                spread_sums = rows_box(spreads[which * LEVELS + level - 1], base, shift, shift, count, first, last)
                if level < LEVELS:
                    grown_sums = rows_box(parts[which * LEVELS + level], base, 0, 0, count, first, last)
                for x in range(count):
                    ok = index < column_limit(x, level)
                    spread = next(spread_sums)
                    grown = next(grown_sums) if level < LEVELS else None
                    for h in range(2):
                        off = WIDE - 2 * level
                        inv = inverses[level - 1][x + off, h, pl.ds(base + off, SUBLANES), :]
                        if level < LEVELS:
                            at = REACH - level
                            own = weights[level][x + at, h, pl.ds(base + at, SUBLANES), :]
                            if which:
                                own = own * labels[x + at, h, pl.ds(base + at, SUBLANES), :]
                            part = (own - inv * spread[h]) * inv + grown[h]
                        else:
                            part = inv * inv * -spread[h]
                        parts[which * LEVELS + level - 1][x, h, pl.ds(base, SUBLANES), :] = jnp.where(ok, part, 0.0)

            over_tiles(cols + 2 * level, pull)

        def finish(base, which=which):
            grown_sums = rows_box(parts[which * LEVELS], base, 0, 0, rows, first, last)
            for x, grown in enumerate(grown_sums):
                for h in range(2):
                    power = powers[0][x + WIDE, h, pl.ds(base + WIDE, SUBLANES), :]
                    own = weights[0][x + REACH, h, pl.ds(base + REACH, SUBLANES), :]
                    if which:
                        own = own * labels[x + REACH, h, pl.ds(base + REACH, SUBLANES), :]
                    stage[1 - which, x, pl.ds(base, SUBLANES), h * LANES : (h + 1) * LANES] = power * grown[h] + own

        for tile in range(tiles_for(cols)):
            finish(tile * SUBLANES)
            copies[1 - which][tile].start()

    totals = [jnp.zeros((SUBLANES, LANES), jnp.float32) for _ in range(4)]
    for base in range(0, cols, SUBLANES):
        for x in range(rows):
            for h in range(2):
                half = slice(h * LANES, (h + 1) * LANES)
                skel = skels[x + REACH, h, pl.ds(base + REACH, SUBLANES), :]
                other = mask_skel[x, pl.ds(base, SUBLANES), half]
                totals[0] += skel * labels[x + REACH, h, pl.ds(base + REACH, SUBLANES), :]
                totals[1] += skel
                totals[2] += other * own_pred[x, pl.ds(base, SUBLANES), half]
                totals[3] += other
    totals = [jnp.sum(jnp.sum(v, 0, keepdims=True), 1, keepdims=True) for v in totals]
    packed = jnp.broadcast_to(jnp.concatenate(totals * 2, 0), (SUBLANES, LANES))
    for i in range(sums.shape[0] // SUBLANES):
        sums[i * SUBLANES : (i + 1) * SUBLANES, :] = packed
    for copy in sum(copies, []):
        copy.wait()


def combine_kernel(cells, got, results, gradient, loss):
    total = jnp.zeros((SUBLANES, LANES), jnp.float32)
    for i in range(got.shape[0] // SUBLANES):
        total += got[i * SUBLANES : (i + 1) * SUBLANES, :]
    total = total + pltpu.roll(total, 4, 0)
    intersection_pred, mass_pred, intersection_mask, mass_mask = (total[i : i + 1] + 1.0 for i in range(4))
    precision = intersection_pred / mass_pred
    sensitivity = intersection_mask / mass_mask
    paired = precision + sensitivity
    loss[0] = (1.0 - 2.0 * precision * sensitivity / paired)[0, 0]
    slope_prec = -2.0 * sensitivity * sensitivity / (paired * paired)
    slope_sens = -2.0 * precision * precision / (paired * paired)
    coef_intersection = cells * slope_prec / mass_pred
    coef_mass = -coef_intersection * precision
    coef_cross = cells * slope_sens / mass_mask
    a, b, c = (
        jnp.broadcast_to(jnp.concatenate([v, v], 1), (gradient.shape[1], 2 * LANES))
        for v in (coef_intersection, coef_mass, coef_cross)
    )
    for x in range(gradient.shape[0]):
        gradient[x] = a * results[0, x] + b * results[1, x] + c * results[2, x]


def local(prediction, vessel_mask):
    rows, cols, depth = prediction.shape
    none = (0, 0)
    packed = lax.optimization_barrier(
        jnp.pad(prediction, ((0, rows), none, none)) + jnp.pad(vessel_mask, ((rows, 0), none, none)).astype(jnp.float32)
    )
    gx, gy = lax.axis_size("gx"), lax.axis_size("gy")
    halo = with_halo(packed, rows)

    def held(width, margin=2):
        return pltpu.VMEM((rows + 2 * width, 2, tiles_for(cols + 2 * width + margin + 6) * SUBLANES, LANES), jnp.float32)

    scratch = (
        [held(WIDE - k) for k in range(LEVELS + 1)]
        + [held(WIDE - k) for k in range(1, LEVELS + 1)]
        + [held(REACH)] * 4
        + [held(REACH)] * 4
        + [held(REACH)] * 8
        + [held(k) for k in range(1, LEVELS + 1)] * 2
        + [held(REACH)] * 2
        + [held(REACH - k) for k in range(LEVELS + 1)]
        + [held(REACH - k) for k in range(1, LEVELS + 1)]
        + [held(0)] * 4
        + [pltpu.VMEM((3, rows, cols, depth), jnp.float32), pltpu.SemaphoreType.DMA((3, tiles_for(cols)))]
    )
    block = jax.ShapeDtypeStruct((rows, cols, depth), jnp.float32)
    vmem = pl.BlockSpec(memory_space=pltpu.VMEM)
    smem = pl.BlockSpec(memory_space=pltpu.SMEM)
    results, sums = pl.pallas_call(
        lambda *refs: skeleton_kernel(rows, cols, *refs),
        out_shape=[jax.ShapeDtypeStruct((KEPT, rows, cols, depth), jnp.float32), jax.ShapeDtypeStruct((gx * gy * 4, LANES), jnp.float32)],
        in_specs=[vmem] * 5,
        out_specs=[pl.BlockSpec(memory_space=pltpu.HBM), vmem],
        scratch_shapes=scratch,
        compiler_params=pltpu.CompilerParams(vmem_limit_bytes=VMEM_BYTES),
        name="skeleton",
    )(packed[:rows], *halo)
    got = lax.all_to_all(sums, ("gx", "gy"), 0, 0, tiled=True)
    gradient, loss = pl.pallas_call(
        lambda *refs: combine_kernel(float(gx * rows * gy * cols * depth), *refs),
        out_shape=[block, jax.ShapeDtypeStruct((1,), jnp.float32)],
        grid=(1,),
        in_specs=[
            pl.BlockSpec(got.shape, lambda i: (0, 0)),
            pl.BlockSpec((3, rows, cols, depth), lambda i: (0, 0, 0, 0)),
        ],
        out_specs=[pl.BlockSpec(block.shape, lambda i: (0, 0, 0)), smem],
        name="combine",
    )(got, results)
    return (gradient, loss[0])


def solution(mesh):
    placed = (P("gx", "gy", None), P("gx", "gy", None))
    return jax.shard_map(
        local, mesh=mesh, in_specs=placed, out_specs=(P("gx", "gy", None), P()), check_vma=False
    )
```

```python
import jax
import jax.numpy as jnp
from jax import lax
from jax.experimental import pallas as pl
from jax.experimental.pallas import tpu as pltpu
from jax.sharding import PartitionSpec as P

ITERS = 3
LEVELS = ITERS + 1
REACH = LEVELS + 1
softness_factor = 0.1


def moved(block, axis, target):
    count = lax.axis_size(axis)
    pairs = [(i, target(i)) for i in range(count) if 0 <= target(i) < count]
    return lax.ppermute(block, axis, pairs)


def with_halo(packed, rows):
    wide, thin = 2 * REACH, REACH
    rest = wide - rows
    own_pred, own_mask = packed[:rows], packed[rows:]
    spot = lax.axis_index("gx")
    odd, upper = lax.rem(spot, 2) == 1, lax.rem(spot, 4) >= 2
    to_up = jnp.concatenate([own_pred, own_mask[rows - thin :]], 0)
    to_down = jnp.concatenate([own_pred, own_mask[:thin]], 0)
    to_far_up, to_far_down = own_pred[rows - rest :], own_pred[:rest]
    a, b, c, d = lax.optimization_barrier(
        (
            jnp.where(odd, to_down, to_up),
            jnp.where(odd, to_up, to_down),
            jnp.where(upper, to_far_down, to_far_up),
            jnp.where(upper, to_far_up, to_far_down),
        )
    )
    a = moved(a, "gx", lambda i: i ^ 1)
    b = moved(b, "gx", lambda i: i + 1 if i % 2 else i - 1)
    c = moved(c, "gx", lambda i: i ^ 2)
    d = moved(d, "gx", lambda i: i + 2 if i % 4 >= 2 else i - 2)
    a, b, c, d = lax.optimization_barrier((a, b, c, d))
    up, down = jnp.where(odd, a, b), jnp.where(odd, b, a)
    far_up, far_down = jnp.where(upper, c, d), jnp.where(upper, d, c)
    tall_pred = jnp.concatenate([far_up, up[:rows], own_pred, down[:rows], far_down], 0)
    tall_mask = jnp.concatenate([up[rows:], own_mask, down[rows:]], 0)
    tall, short = tall_pred.shape[0], tall_mask.shape[0]

    def side(p, m):
        flat = jnp.concatenate([p.reshape(tall * wide, -1), m.reshape(short * thin, -1)], 0)
        return jnp.pad(flat, ((0, -flat.shape[0] % SUBLANES), (0, 0)))

    col_odd = lax.rem(lax.axis_index("gy"), 2) == 1
    high = side(tall_pred[:, -wide:], tall_mask[:, -thin:])
    low = side(tall_pred[:, :wide], tall_mask[:, :thin])
    first = moved(jnp.where(col_odd, low, high), "gy", lambda i: i ^ 1)
    second = moved(jnp.where(col_odd, high, low), "gy", lambda i: i + 1 if i % 2 else i - 1)
    first, second = lax.optimization_barrier((first, second))
    return tall_pred, tall_mask, jnp.where(col_odd, first, second), jnp.where(col_odd, second, first)


WIDE = 2 * REACH
LANES = 128
SUBLANES = 8
SHARE = LANES // 4
VMEM_BYTES = 40 * 1024 * 1024
KEPT = 210


def tiles_for(count):
    return -(-count // SUBLANES)


def depth_sum(low, high, first, last):
    low_up, high_up = pltpu.roll(low, 1, 1), pltpu.roll(high, 1, 1)
    low_down, high_down = pltpu.roll(low, LANES - 1, 1), pltpu.roll(high, LANES - 1, 1)
    return (
        low + jnp.where(first, 0.0, low_up) + jnp.where(last, high_down, low_down),
        high + jnp.where(first, low_up, high_up) + jnp.where(last, 0.0, high_down),
    )


def rows_box(ref, base, row_shift, col_shift, count, first, last):
    def across(x, h):
        parts = [ref[x + row_shift, h, pl.ds(base + (col_shift + d), SUBLANES), :] for d in range(3)]
        return parts[0] + parts[1] + parts[2]

    rows = [[across(x, h) for h in range(2)] for x in range(2)]
    for x in range(0, count, 2):
        rows += [[across(x + d, h) for h in range(2)] for d in (2, 3)]
        shared = [rows[1][h] + rows[2][h] for h in range(2)]
        yield depth_sum(*(rows[0][h] + shared[h] for h in range(2)), first, last)
        yield depth_sum(*(shared[h] + rows[3][h] for h in range(2)), first, last)
        rows = rows[2:]


def over_tiles(count, step):
    def body(i, carry):
        step(i * SUBLANES)
        return carry

    lax.fori_loop(0, tiles_for(count), body, 0, unroll=True)


def skeleton_kernel(rows, cols, own_pred, pred, label, left, right, results, sums, *scratch):
    t = softness_factor
    scratch = list(scratch)
    stage, copied = scratch[48:]
    mask_skel = stage.at[2]
    tiles = [pl.ds(base, SUBLANES) for base in range(0, cols, SUBLANES)]
    copies = [
        [pltpu.make_async_copy(stage.at[i, :, t], results.at[i, :, t], copied.at[i, n]) for n, t in enumerate(tiles)]
        for i in range(3)
    ]
    powers = scratch[:5]
    inverses = scratch[5:9]
    opened = scratch[9:13]
    weights = scratch[13:17]
    spreads = scratch[17:25]
    parts = scratch[25:33]
    labels, skels = scratch[33:35]
    label_powers = scratch[35:40]
    label_inverses = scratch[40:44]
    label_opened = scratch[44:48]
    row0, row_count = lax.axis_index("gx") * rows, lax.axis_size("gx") * rows
    col0, col_count = lax.axis_index("gy") * cols, lax.axis_size("gy") * cols
    lane = lax.broadcasted_iota(jnp.int32, (SUBLANES, LANES), 1)
    sublane = lax.broadcasted_iota(jnp.int32, (SUBLANES, LANES), 0)
    first, last = lane == 0, lane == LANES - 1

    def column_index(base, width):
        index = sublane + (base + (col0 - width))
        return jnp.where(index < 0, 1 << 20, index)

    def column_limit(x, width):
        row = row0 + (x - width)
        return jnp.where((row >= 0) & (row < row_count), col_count, 0)

    def raise_field(middle, offset, powers, inverses, width, kept=None):
        last_tile = max(width - SUBLANES, 0)
        sides = (0, last_tile) if last_tile else (0,)
        tiles = [(at, left, at) for at in sides]
        tiles += [(width + at, None, at) for at in range(0, cols, SUBLANES)]
        tiles += [(width + cols + at, right, at) for at in sides]
        indices = [column_index(base, width) for base, _, _ in tiles]
        for x in range(rows + 2 * width):
            limit = column_limit(x, width)
            for (base, source, at), index in zip(tiles, indices):
                ok = index < limit
                for h in range(2):
                    half = slice(h * LANES, (h + 1) * LANES)
                    if source is None:
                        value = middle[x, at : at + SUBLANES, half]
                    else:
                        row = offset + x * width + at
                        value = source[row : row + SUBLANES, half]
                    if kept is not None:
                        kept[x, h, pl.ds(base, SUBLANES), :] = value
                    powers[0][x, h, pl.ds(base, SUBLANES), :] = jnp.where(ok, jnp.exp(value * (-1.0 / t)), 0.0)

        for level in range(1, LEVELS + 1):
            here = width - level

            def erode(base, level=level, here=here):
                index = column_index(base, here)
                sums_of = rows_box(powers[level - 1], base, 0, 0, rows + 2 * here, first, last)
                for x, pair in enumerate(sums_of):
                    ok = index < column_limit(x, here)
                    for h in range(2):
                        if level < LEVELS:
                            powers[level][x, h, pl.ds(base, SUBLANES), :] = jnp.where(ok, pair[h], 0.0)
                        inverses[level - 1][x, h, pl.ds(base, SUBLANES), :] = jnp.where(ok, 1.0 / pair[h], 0.0)

            over_tiles(cols + 2 * here, erode)

    def open_field(inverses, opened, width, keep):
        for level in range(1, LEVELS + 1):
            shift = width - level - keep - 1

            def dilate(base, level=level, shift=shift):
                sums_of = rows_box(inverses[level - 1], base, shift, shift, rows + 2 * keep, first, last)
                for x, pair in enumerate(sums_of):
                    for h in range(2):
                        opened[level - 1][x, h, pl.ds(base, SUBLANES), :] = pair[h]

            over_tiles(cols + 2 * keep, dilate)

    def chain(power_of, opened_of):
        skel, saved = None, []
        for j in range(LEVELS):
            wide = opened_of(j)
            product = power_of(j) * wide
            over = 1.0 / (wide * (1.0 + product))
            slope = wide * over
            delta = -jnp.log(product * slope)
            if skel is None:
                skel = delta
                saved.append((slope, over, delta, None, None))
            else:
                left = 1.0 - t * skel
                e = jnp.exp(delta * left)
                grown = 1.0 + e
                saved.append((slope, over, delta, left, e / grown))
                skel = skel + jnp.log(grown)
        return skel, saved

    raise_field(label, (rows + 2 * WIDE) * WIDE, label_powers, label_inverses, REACH, labels)
    open_field(label_inverses, label_opened, REACH, 0)

    def label_chain(base):
        for x in range(rows):
            for h in range(2):
                skel, _ = chain(
                    lambda j: label_powers[j][x + REACH - j, h, pl.ds(base + (REACH - j), SUBLANES), :],
                    lambda j: label_opened[j][x, h, pl.ds(base, SUBLANES), :],
                )
                mask_skel[x, pl.ds(base, SUBLANES), h * LANES : (h + 1) * LANES] = t * skel

    over_tiles(cols, label_chain)
    for copy in copies[2]:
        copy.start()

    raise_field(pred, 0, powers, inverses, WIDE)
    open_field(inverses, opened, WIDE, REACH)

    def chain_tile(base):
        index = column_index(base, REACH)
        for x in range(rows + 2 * REACH):
            away = max(REACH - x, x - REACH - rows + 1)
            ok = index < column_limit(x, REACH)
            for h in range(2):
                skel, saved = chain(
                    lambda j: powers[j][x + REACH - j, h, pl.ds(base + (REACH - j), SUBLANES), :],
                    lambda j: opened[j][x, h, pl.ds(base, SUBLANES), :],
                )
                if away <= 0:
                    skels[x, h, pl.ds(base, SUBLANES), :] = t * skel
                seed = labels[x, h, pl.ds(base, SUBLANES), :]
                rest = jnp.where(ok, 1.0, 0.0)
                for j in range(ITERS, max(0, away - 2) - 1, -1):
                    slope, over, delta, left, rect = saved[j]
                    if j:
                        inner = rest * rect
                        scaled = inner * left
                        rest = rest - inner * (t * delta)
                    else:
                        scaled = rest
                    if away <= j:
                        weights[j][x, h, pl.ds(base, SUBLANES), :] = jnp.where(ok, scaled * slope, 0.0)
                    spread = jnp.where(ok, scaled * over, 0.0)
                    spreads[j][x, h, pl.ds(base, SUBLANES), :] = spread
                    spreads[LEVELS + j][x, h, pl.ds(base, SUBLANES), :] = seed * spread

    over_tiles(cols + 2 * REACH, chain_tile)

    for which in range(2):
        for level in range(LEVELS, 0, -1):

            def pull(base, level=level, which=which):
                index = column_index(base, level)
                count = rows + 2 * level
                shift = REACH - level - 1
                spread_sums = rows_box(spreads[which * LEVELS + level - 1], base, shift, shift, count, first, last)
                if level < LEVELS:
                    grown_sums = rows_box(parts[which * LEVELS + level], base, 0, 0, count, first, last)
                for x in range(count):
                    ok = index < column_limit(x, level)
                    spread = next(spread_sums)
                    grown = next(grown_sums) if level < LEVELS else None
                    for h in range(2):
                        off = WIDE - 2 * level
                        inv = inverses[level - 1][x + off, h, pl.ds(base + off, SUBLANES), :]
                        if level < LEVELS:
                            at = REACH - level
                            own = weights[level][x + at, h, pl.ds(base + at, SUBLANES), :]
                            if which:
                                own = own * labels[x + at, h, pl.ds(base + at, SUBLANES), :]
                            part = (own - inv * spread[h]) * inv + grown[h]
                        else:
                            part = inv * inv * -spread[h]
                        parts[which * LEVELS + level - 1][x, h, pl.ds(base, SUBLANES), :] = jnp.where(ok, part, 0.0)

            over_tiles(cols + 2 * level, pull)

        def finish(base, which=which):
            grown_sums = rows_box(parts[which * LEVELS], base, 0, 0, rows, first, last)
            for x, grown in enumerate(grown_sums):
                for h in range(2):
                    power = powers[0][x + WIDE, h, pl.ds(base + WIDE, SUBLANES), :]
                    own = weights[0][x + REACH, h, pl.ds(base + REACH, SUBLANES), :]
                    if which:
                        own = own * labels[x + REACH, h, pl.ds(base + REACH, SUBLANES), :]
                    stage[1 - which, x, pl.ds(base, SUBLANES), h * LANES : (h + 1) * LANES] = power * grown[h] + own

        for tile in range(tiles_for(cols)):
            finish(tile * SUBLANES)
            copies[1 - which][tile].start()

    totals = [jnp.zeros((SUBLANES, LANES), jnp.float32) for _ in range(4)]
    for base in range(0, cols, SUBLANES):
        for x in range(rows):
            for h in range(2):
                half = slice(h * LANES, (h + 1) * LANES)
                skel = skels[x + REACH, h, pl.ds(base + REACH, SUBLANES), :]
                other = mask_skel[x, pl.ds(base, SUBLANES), half]
                totals[0] += skel * labels[x + REACH, h, pl.ds(base + REACH, SUBLANES), :]
                totals[1] += skel
                totals[2] += other * own_pred[x, pl.ds(base, SUBLANES), half]
                totals[3] += other
    totals = [jnp.sum(jnp.sum(v, 0, keepdims=True), 1, keepdims=True) for v in totals]
    packed = jnp.zeros((SUBLANES, LANES), jnp.float32)
    for i, total in enumerate(totals):
        packed = jnp.where(lane // SHARE == i, total, packed)
    for i in range(sums.shape[0] // SUBLANES):
        sums[i * SUBLANES : (i + 1) * SUBLANES, :] = packed
    for copy in sum(copies, []):
        copy.wait()


def combine_kernel(cells, got, results, gradient, loss):
    total = jnp.zeros((SUBLANES, LANES), jnp.float32)
    for i in range(got.shape[0] // SUBLANES):
        total += got[i * SUBLANES : (i + 1) * SUBLANES, :]
    total = jnp.sum(total, 0, keepdims=True)
    share = lax.broadcasted_iota(jnp.int32, (1, LANES), 1) // SHARE
    intersection_pred, mass_pred, intersection_mask, mass_mask = (
        jnp.sum(jnp.where(share == i, total, 0.0), 1, keepdims=True) * (1.0 / SHARE) + 1.0 for i in range(4)
    )
    precision = intersection_pred / mass_pred
    sensitivity = intersection_mask / mass_mask
    paired = precision + sensitivity
    loss[0] = (1.0 - 2.0 * precision * sensitivity / paired)[0, 0]
    slope_prec = -2.0 * sensitivity * sensitivity / (paired * paired)
    slope_sens = -2.0 * precision * precision / (paired * paired)
    coef_intersection = cells * slope_prec / mass_pred
    coef_mass = -coef_intersection * precision
    coef_cross = cells * slope_sens / mass_mask
    a, b, c = (
        jnp.broadcast_to(v, (gradient.shape[1], 2 * LANES))
        for v in (coef_intersection, coef_mass, coef_cross)
    )
    for x in range(gradient.shape[0]):
        gradient[x] = a * results[0, x] + b * results[1, x] + c * results[2, x]


def local(prediction, vessel_mask):
    rows, cols, depth = prediction.shape
    none = (0, 0)
    packed = lax.optimization_barrier(
        jnp.pad(prediction, ((0, rows), none, none)) + jnp.pad(vessel_mask, ((rows, 0), none, none)).astype(jnp.float32)
    )
    gx, gy = lax.axis_size("gx"), lax.axis_size("gy")
    halo = with_halo(packed, rows)

    def held(width, margin=2):
        return pltpu.VMEM((rows + 2 * width, 2, tiles_for(cols + 2 * width + margin + 6) * SUBLANES, LANES), jnp.float32)

    scratch = (
        [held(WIDE - k) for k in range(LEVELS + 1)]
        + [held(WIDE - k) for k in range(1, LEVELS + 1)]
        + [held(REACH)] * 4
        + [held(REACH)] * 4
        + [held(REACH)] * 8
        + [held(k) for k in range(1, LEVELS + 1)] * 2
        + [held(REACH)] * 2
        + [held(REACH - k) for k in range(LEVELS + 1)]
        + [held(REACH - k) for k in range(1, LEVELS + 1)]
        + [held(0)] * 4
        + [pltpu.VMEM((3, rows, cols, depth), jnp.float32), pltpu.SemaphoreType.DMA((3, tiles_for(cols)))]
    )
    block = jax.ShapeDtypeStruct((rows, cols, depth), jnp.float32)
    vmem = pl.BlockSpec(memory_space=pltpu.VMEM)
    smem = pl.BlockSpec(memory_space=pltpu.SMEM)
    results, sums = pl.pallas_call(
        lambda *refs: skeleton_kernel(rows, cols, *refs),
        out_shape=[jax.ShapeDtypeStruct((KEPT, rows, cols, depth), jnp.float32), jax.ShapeDtypeStruct((gx * gy, LANES), jnp.float32)],
        in_specs=[vmem] * 5,
        out_specs=[pl.BlockSpec(memory_space=pltpu.HBM), vmem],
        scratch_shapes=scratch,
        compiler_params=pltpu.CompilerParams(vmem_limit_bytes=VMEM_BYTES),
        name="skeleton",
    )(packed[:rows], *halo)
    got = lax.all_to_all(sums, ("gx", "gy"), 0, 0, tiled=True)
    gradient, loss = pl.pallas_call(
        lambda *refs: combine_kernel(float(gx * rows * gy * cols * depth), *refs),
        out_shape=[block, jax.ShapeDtypeStruct((1,), jnp.float32)],
        grid=(1,),
        in_specs=[
            pl.BlockSpec(got.shape, lambda i: (0, 0)),
            pl.BlockSpec((3, rows, cols, depth), lambda i: (0, 0, 0, 0)),
        ],
        out_specs=[pl.BlockSpec(block.shape, lambda i: (0, 0, 0)), smem],
        name="combine",
    )(got, results)
    return (gradient, loss[0])


def solution(mesh):
    placed = (P("gx", "gy", None), P("gx", "gy", None))
    return jax.shard_map(
        local, mesh=mesh, in_specs=placed, out_specs=(P("gx", "gy", None), P()), check_vma=False
    )
```
